32 devices in a mesh: grp: 2 (over x), comp: 8 (over z, y), lev: 2 (over core).
Axes of the slice: x: 2, y: 2, z: 4, core: 2. Of those that a mesh axis runs over, the one named last changes fastest.
Arguments:
- atm_state: float32 [4, 72, 65536], P(None, 'lev', ('grp', 'comp')), parts along dimension 2, may hold values from -6 to 6
- ocn_state: float32 [4, 80, 65536], P(None, 'lev', ('grp', 'comp')), parts along dimension 2, may hold values from -6 to 6
- atm_weights: float32 [72], P('lev'), may hold values from 0.02 to 0.2
- ocn_weights: float32 [80], P('lev'), may hold values from 0.02 to 0.2
- atm_metric: float32 [4, 32768], P(None, 'comp'), may hold values from 0.05 to 0.25
- ocn_metric: float32 [6, 32768], P(None, 'comp'), may hold values from 0.03 to 0.15
- atm_links: int32 [4, 32768], P(None, 'comp'), may hold values from 0 to 32767, as said below
- ocn_links: int32 [6, 32768], P(None, 'comp'), may hold values from 0 to 32767, as said below
- tile_weights: bfloat16 [1024, 128, 128], P(('comp', 'lev')), may hold values from -0.5 to 0.5
- tile_source: int32 [1024], P(('comp', 'lev')), may hold values from 0 to 63
- tile_target: int32 [1024], P(('comp', 'lev')), may hold values from 0 to 255, as said below
- owner_map: int32 [256], replicated, may hold values from 0 to 255, as said below
Outputs:
- atm_new: float32 [4, 72, 65536], P(None, 'lev', ('grp', 'comp')), parts along dimension 2
- ocn_new: float32 [4, 80, 65536], P(None, 'lev', ('grp', 'comp')), parts along dimension 2
- xgrid_flux: bfloat16 [512, 8, 128], P(('grp', 'comp', 'lev')), parts along dimension 0
The draws below stay inside these ranges and needn't reach their ends.
There are 2 independent parts, one for each index of `grp`. The reference program is written for one: setup_inputs(seed, part) draws one part's arguments, and reference() takes and returns one part's arrays. A program takes and returns all parts, laid end to end along the dimension named above; an argument that names none is the same for every part. Nothing has to cross between parts.
Inputs may be any that keep to these rules, and one draw needn't show every extreme that they name: `atm_links`: each column's neighbour lies at most 128 columns away along the strip of 32768 columns, wrapping at its ends, and never at distance 0; distances 128 and -128 both occur. `ocn_links`: each cell's neighbour lies at most 128 cells away along the strip of 32768 cells, wrapping at its ends, and never at distance 0; distances 128 and -128 both occur. Each value once; the owner of block s is the device owner_map[s] // 16 of comp+lev. `tile_target`: of the tiles of one device at most 4 have targets of one owner, and in every draw one owner receives exactly 4 tiles from every device.
All inputs are finite; a program needn't handle non-finite values.
Results may differ from the reference program's by a relative error of at most 0.0052.
Values may be sent and summed in bfloat16 or wider, within the bound.
No kernel may reach another device: no remote copies, remote signals or barrier semaphores. Data moves between devices by JAX's collectives and lax.ppermute only.
A program may use at most 128 MiB of HBM per device.

```python
import math
import jax
import jax.numpy as jnp
from jax import lax

FIELDS = 4
LEVA = 72
LEVO = 80
TILE = 128
BLK_DEV = 32
KA = 4
KO = 6
HALO = 128
TILE_DEV = 64
CAP = 4
XB_DEV = 16
NCOLS = 32768
TILES = 1024
XBLOCKS = 256
N_COMP = 8
N_LEV = 2


def tile_plan(key):
    devices = TILES // TILE_DEV
    slot_count = devices * CAP
    key_perm, key_rank, key_score, key_block, key_shuffle = jax.random.split(key, 5)
    positions = jax.random.permutation(key_perm, XBLOCKS).astype(jnp.int32)
    blocks_at = jnp.argsort(positions).astype(jnp.int32)
    hotness = jax.random.permutation(key_rank, devices).astype(jnp.int32)
    owner_of_slot = jnp.arange(slot_count, dtype=jnp.int32) // CAP
    random_part = jax.random.randint(key_score, (devices, slot_count), 0, 4096)
    lifted = jnp.where(hotness[owner_of_slot] < max(devices // 8, 1), 4096, 0)
    forced = jnp.where(hotness[owner_of_slot] == 0, 65536, 0)
    scores = (random_part + lifted[None, :] + forced[None, :]) * slot_count + jnp.arange(slot_count, dtype=jnp.int32)[None, :]
    scores_top, chosen = lax.top_k(scores, TILE_DEV)
    chosen = jax.random.permutation(key_shuffle, chosen, axis=1, independent=True)
    owners = chosen // CAP
    in_owner = jax.random.randint(key_block, (devices, TILE_DEV), 0, XB_DEV)
    target = jnp.take(blocks_at, (owners * XB_DEV + in_owner).reshape(-1))
    return (positions, target.astype(jnp.int32))


def strip_links(key, count):
    key_size, key_sign = jax.random.split(key, 2)
    distance = jax.random.randint(key_size, (count, NCOLS), 1, HALO + 1)
    sign_pick = 2 * jax.random.randint(key_sign, (count, NCOLS), 0, 2) - 1
    offset = distance * sign_pick
    offset = offset.at[0, 0].set(HALO).at[1, 0].set(-HALO)
    columns = jnp.arange(NCOLS, dtype=jnp.int32)[None, :]
    return ((columns + offset) % NCOLS).astype(jnp.int32)


def draw_owner_map(key, part):
    return tile_plan(key)[0]


def draw_tile_target(key, part):
    return tile_plan(key)[1]


def draw_atm_links(key, part):
    key = jax.random.fold_in(key, 5)
    return strip_links(key, KA)


def draw_ocn_links(key, part):
    key = jax.random.fold_in(key, 6)
    return strip_links(key, KO)


def place_ends(drawn, own_key, least, largest):
    longest = drawn.shape.index(max(drawn.shape))
    spots = []
    for shift in (0, 1):
        where = [jax.random.randint(jax.random.fold_in(own_key, axis), (), 0, length) for axis, length in enumerate(drawn.shape)]
        where[longest] = (where[longest] + shift) % drawn.shape[longest]
        spots.append(tuple(where))
    return drawn.at[spots[0]].set(least).at[spots[1]].set(largest)


def steps_of(stream_key, shape, pieces, least, top_value):
    def one(dim, parts):
        draws = jax.random.uniform(jax.random.fold_in(jax.random.fold_in(stream_key, 6), dim), (parts,), jnp.float32, least / len(pieces), top_value / len(pieces))
        return jnp.repeat(jnp.exp(draws), shape[dim] // parts).reshape((-1,) + (1,) * (len(shape) - dim - 1))

    gain = one(*pieces[0])
    for cut in pieces[1:]:
        gain = gain * one(*cut)
    return gain


def centred(rng, shape, spread, bound, cuts=(), held_as=jnp.bfloat16):
    level = steps_of(rng, shape, cuts, -0.22, 0.18) if cuts else 1.0
    array = jax.random.normal(rng, shape, jnp.float32) * spread * level
    return jnp.minimum(jnp.maximum(array, -bound), bound).astype(held_as)


def setup_inputs(seed: int = 0, part: int = 0) -> dict:
    streams_of = jax.random.split(jax.random.key(seed), 13)
    part_splits = jax.random.split(jax.random.fold_in(streams_of[12], part), 13)
    return {
        "atm_state": centred(part_splits[0], (FIELDS, LEVA, NCOLS), 1.0, 6.0, ((1, 2), (2, 8)), jnp.float32),
        "ocn_state": centred(part_splits[1], (FIELDS, LEVO, NCOLS), 1.0, 6.0, ((1, 2), (2, 8)), jnp.float32),
        "atm_weights": jnp.clip(jnp.exp(math.log(0.2) - 2.3025851 * jax.random.uniform(streams_of[2], (LEVA,), jnp.float32) ** steps_of(streams_of[2], (LEVA,), ((0, 2),), -0.2, 0.2)), 0.02, 0.2),
        "ocn_weights": jnp.clip(jnp.exp(math.log(0.2) - 2.3025851 * jax.random.uniform(streams_of[3], (LEVO,), jnp.float32) ** steps_of(streams_of[3], (LEVO,), ((0, 2),), -0.2, 0.2)), 0.02, 0.2),
        "atm_metric": jnp.clip(jnp.exp(math.log(0.25) - 1.609438 * jax.random.uniform(streams_of[4], (KA, NCOLS), jnp.float32) ** steps_of(streams_of[4], (KA, NCOLS), ((1, 8),), -0.2, 0.2)), 0.05, 0.25),
        "ocn_metric": jnp.clip(jnp.exp(math.log(0.15) - 1.609438 * jax.random.uniform(streams_of[5], (KO, NCOLS), jnp.float32) ** steps_of(streams_of[5], (KO, NCOLS), ((1, 8),), -0.2, 0.2)), 0.03, 0.15),
        "atm_links": draw_atm_links(jax.random.fold_in(streams_of[12], 71), part),
        "ocn_links": draw_ocn_links(jax.random.fold_in(streams_of[12], 71), part),
        "tile_weights": centred(streams_of[8], (TILES, TILE, TILE), TILE ** -0.5, 0.5, ((0, 16),)),
        "tile_source": place_ends(jax.random.randint(streams_of[9], (TILES,), 0, 2 * BLK_DEV), jax.random.fold_in(streams_of[9], 1), 0, (2 * BLK_DEV) - 1).astype(jnp.int32),
        "tile_target": draw_tile_target(jax.random.fold_in(streams_of[12], 71), part),
        "owner_map": draw_owner_map(jax.random.fold_in(streams_of[12], 71), part),
    }


step_size = 1.0
flux_gain = 10.0

def bulk_fluxes(atm_side, ocn_side):
    temp_air = atm_side[..., 0, :]
    humid_air = atm_side[..., 1, :]
    wind_u = atm_side[..., 2, :]
    wind_v = atm_side[..., 3, :]
    temp_sea = ocn_side[..., 0, :]
    salt_sea = ocn_side[..., 1, :]
    current_u = ocn_side[..., 2, :]
    current_v = ocn_side[..., 3, :]
    shear_u = wind_u - current_u
    shear_v = wind_v - current_v
    wind_speed = jnp.sqrt(shear_u * shear_u + shear_v * shear_v + 1.0)
    stress_u = 0.8 * wind_speed * shear_u
    stress_v = 0.8 * wind_speed * shear_v
    sensible = 0.6 * wind_speed * (temp_sea - temp_air)
    saturated = 0.6 * jnp.exp(0.3 * temp_sea) * (1.0 - 0.1 * jnp.tanh(salt_sea))
    latent = 0.5 * wind_speed * (saturated - humid_air)
    atm_flux = jnp.stack([sensible, latent, -stress_u, -stress_v], axis=-2)
    ocn_flux = jnp.stack([-(sensible + latent), latent, stress_u, stress_v], axis=-2)
    return (atm_flux, ocn_flux)

def diffuse(field_state, metric, neighbours):
    result = jnp.zeros_like(field_state)
    for edge in range(neighbours.shape[0]):
        beside = jnp.take(field_state, neighbours[edge], axis=2)
        result = result + metric[edge][None, None, :] * (beside - field_state)
    return result

def reference(atm_state, ocn_state, atm_weights, ocn_weights, atm_metric, ocn_metric, atm_links, ocn_links, tile_weights, tile_source, tile_target, owner_map):
    highest = lax.Precision.HIGHEST
    surf_atm = jnp.einsum('flc,l->fc', atm_state, atm_weights, precision=highest)
    surf_ocn = jnp.einsum('flc,l->fc', ocn_state, ocn_weights, precision=highest)
    blocks = jnp.concatenate([surf_atm.reshape(FIELDS, N_COMP, BLK_DEV, TILE), surf_ocn.reshape(FIELDS, N_COMP, BLK_DEV, TILE)], axis=2).astype(jnp.bfloat16)
    comp_of = (jnp.arange(TILES) // (TILE_DEV * N_LEV)).astype(jnp.int32)
    source_rows = blocks[:, comp_of, tile_source, :].astype(jnp.float32)
    weights_wide = tile_weights.astype(jnp.float32)
    contrib = jnp.einsum('fti,tij->tfj', source_rows, weights_wide, precision=highest)
    is_ocean = (tile_source >= BLK_DEV).astype(jnp.int32)
    segment = (is_ocean * XBLOCKS + tile_target).astype(jnp.int32)
    xsum = jax.ops.segment_sum(contrib, segment, num_segments=2 * XBLOCKS)
    atm_flux, ocn_flux = bulk_fluxes(xsum[:XBLOCKS], xsum[XBLOCKS:])
    atm_flux = atm_flux.astype(jnp.bfloat16)
    ocn_flux = ocn_flux.astype(jnp.bfloat16)
    xgrid_flux = jnp.zeros((XBLOCKS, 2 * FIELDS, TILE), jnp.bfloat16).at[owner_map].set(jnp.concatenate([atm_flux, ocn_flux], axis=1))
    table = jnp.concatenate([atm_flux, ocn_flux], axis=0)
    tile_flux = table[segment].astype(jnp.float32)
    back = jnp.einsum('tfj,tij->tfi', tile_flux, weights_wide, precision=highest)
    source_id = (comp_of * (2 * BLK_DEV) + tile_source).astype(jnp.int32)
    per_block = jax.ops.segment_sum(back, source_id, num_segments=N_COMP * 2 * BLK_DEV)
    per_block = per_block.reshape(N_COMP, 2 * BLK_DEV, FIELDS, TILE)
    atm_sflux = per_block[:, :BLK_DEV].transpose(2, 0, 1, 3).reshape(FIELDS, NCOLS)
    ocn_sflux = per_block[:, BLK_DEV:].transpose(2, 0, 1, 3).reshape(FIELDS, NCOLS)
    atm_new = atm_state + step_size * diffuse(atm_state, atm_metric, atm_links) + flux_gain * atm_weights[None, :, None] * atm_sflux[:, None, :]
    ocn_new = ocn_state + step_size * diffuse(ocn_state, ocn_metric, ocn_links) + flux_gain * ocn_weights[None, :, None] * ocn_sflux[:, None, :]
    return (atm_new, ocn_new, xgrid_flux)
```

```python
import functools

import jax
import jax.numpy as jnp
from jax import lax
from jax.experimental import pallas as pl
from jax.experimental.pallas import tpu as pltpu
from jax.sharding import PartitionSpec as P

HALO = 128
CAP = 4
XB_DEV = 16
TILE = 128
step_size = 1.0
flux_gain = 10.0
BF16 = jnp.bfloat16
F32 = jnp.float32
BOTH = ("comp", "lev")


def in_vmem():
    return pl.BlockSpec(memory_space=pltpu.VMEM)


def in_smem():
    return pl.BlockSpec(memory_space=pltpu.SMEM)


def in_hbm():
    return pl.BlockSpec(memory_space=pl.ANY)


def held(array):
    return pltpu.with_memory_space_constraint(array, pltpu.VMEM)


def outside(array):
    return pltpu.with_memory_space_constraint(array, pltpu.HBM)


def limit(mib):
    return pltpu.CompilerParams(vmem_limit_bytes=mib * 1024 * 1024)


def to_rows(state):
    fields, levels, columns = state.shape
    blocks = columns // TILE
    split = state.transpose(1, 0, 2).reshape(levels, fields, blocks, TILE)
    return split.transpose(0, 2, 1, 3).reshape(levels, blocks * fields, TILE)


def from_rows(rows, fields):
    levels, count, _ = rows.shape
    blocks = count // fields
    split = rows.reshape(levels, blocks, fields, TILE).transpose(0, 2, 1, 3)
    return split.reshape(levels, fields, blocks * TILE).transpose(1, 0, 2)


def surface_kernel(
    chunks, atm_hbm, ocn_hbm, atm_w, ocn_w, part_ref, head_ref, tail_ref, atm_wide, ocn_wide, atm_ref, ocn_ref,
    atm_s, ocn_s, sems, few_sems,
):
    levels, atm_rows, _ = atm_ref.shape
    fields, ocn_levels, columns = ocn_ref.shape
    deep = atm_rows // chunks
    wide = columns // chunks
    copies = []
    for chunk in range(chunks):
        rows = pl.ds(chunk * deep, deep)
        cols = pl.ds(chunk * wide, wide)
        for which, (src, dst) in enumerate(
            ((atm_hbm.at[:, rows, :], atm_ref.at[:, rows, :]), (ocn_hbm.at[:, :, cols], ocn_ref.at[:, :, cols]))
        ):
            copy = pltpu.make_async_copy(src, dst, sems.at[chunk, which])
            copy.start()
            copies.append(copy)
    few = [
        pltpu.make_async_copy(atm_w, atm_s, few_sems.at[0]),
        pltpu.make_async_copy(ocn_w, ocn_s, few_sems.at[1]),
    ]
    for copy in few:
        copy.start()
    for copy in few:
        copy.wait()
    for level in range(levels):
        atm_wide[level] = jnp.full((8, TILE), atm_s[level], F32)
    for level in range(ocn_levels):
        ocn_wide[level : level + 1] = jnp.full((1, TILE), ocn_s[level], F32)
    for chunk in range(chunks):
        copies[2 * chunk].wait()
        copies[2 * chunk + 1].wait()

        def one_pair(pair, carry):
            rows = pl.ds(pl.multiple_of(pair * 8, 8), 8)
            atm = atm_ref[0, rows, :] * atm_wide[0]
            for level in range(1, levels):
                atm = atm + atm_ref[level, rows, :] * atm_wide[level]
            for half in range(2):
                block = 2 * pair + half
                cols = pl.ds(pl.multiple_of(block * TILE, TILE), TILE)
                ocn = [
                    jnp.sum(ocn_ref[field, :, cols] * ocn_wide[...], axis=0, keepdims=True) for field in range(fields)
                ]
                part_ref[block] = jnp.concatenate([atm[half * fields : (half + 1) * fields]] + ocn, axis=0)
            return carry

        lax.fori_loop(chunk * (deep // 8), (chunk + 1) * (deep // 8), one_pair, 0)
    for ref, row, col in ((head_ref, 0, 0), (tail_ref, atm_rows - fields, columns - HALO)):
        stack = [atm_ref[level, row : row + fields, :] for level in range(levels)]
        stack += [ocn_ref[field, :, col : col + HALO] for field in range(fields)]
        ref[...] = jnp.concatenate(stack, axis=0).astype(BF16)


def surface(atm_rows, ocn_state, atm_weights, ocn_weights):
    levels, count, _ = atm_rows.shape
    fields, ocn_levels, columns = ocn_state.shape
    rows = fields * (levels + ocn_levels)
    chunks = 4
    return pl.pallas_call(
        functools.partial(surface_kernel, chunks),
        out_shape=(
            jax.ShapeDtypeStruct((columns // TILE, 2 * fields, TILE), F32),
            jax.ShapeDtypeStruct((rows, HALO), BF16),
            jax.ShapeDtypeStruct((rows, HALO), BF16),
            jax.ShapeDtypeStruct((levels, 8, TILE), F32),
            jax.ShapeDtypeStruct((ocn_levels, TILE), F32),
        ),
        in_specs=[in_hbm()] * 4,
        out_specs=(in_vmem(),) * 5,
        scratch_shapes=[
            pltpu.VMEM(atm_rows.shape, F32),
            pltpu.VMEM(ocn_state.shape, F32),
            pltpu.SMEM((levels,), F32),
            pltpu.SMEM((ocn_levels,), F32),
            pltpu.SemaphoreType.DMA((chunks, 2)),
            pltpu.SemaphoreType.DMA((2,)),
        ],
        compiler_params=limit(12),
        name="surface",
    )(outside(atm_rows), outside(ocn_state), outside(atm_weights), outside(ocn_weights))


def contrib_kernel(blocks, source_ref, own_ref, other_ref, weight_ref, select_ref, label_ref, out_ref, surf_ref, row_ref):
    surf_ref[...] = (own_ref[...] + other_ref[...]).astype(BF16).astype(F32)
    tiles = weight_ref.shape[0]
    both = own_ref.shape[1]
    devs, depth, _ = out_ref.shape

    def one_tile(tile, carry):
        block = lax.rem(source_ref[tile], blocks)
        row_ref[pl.ds(pl.multiple_of(both * tile, both), both)] = jnp.dot(
            surf_ref[block].astype(BF16), weight_ref[tile], preferred_element_type=F32
        )
        return carry

    lax.fori_loop(0, tiles, one_tile, 0, unroll=True)
    placed = jnp.dot(select_ref[...], row_ref[...].astype(BF16), preferred_element_type=F32)
    placed = placed.reshape(devs, depth - 8, TILE)
    out_ref[...] = jnp.concatenate([placed, label_ref[...]], axis=1).astype(BF16)


def contributions(own, other, tile_source, tile_weights, select, labels):
    blocks, both, _ = own.shape
    tiles = tile_weights.shape[0]
    devs = labels.shape[0]
    return pl.pallas_call(
        functools.partial(contrib_kernel, blocks),
        out_shape=jax.ShapeDtypeStruct((devs, CAP * both // 2 + 8, TILE), BF16),
        in_specs=[in_smem()] + [in_vmem()] * 5,
        out_specs=in_vmem(),
        scratch_shapes=[pltpu.VMEM(own.shape, F32), pltpu.VMEM((tiles * both, TILE), F32)],
        compiler_params=limit(8),
        name="contributions",
    )(tile_source, own, other, tile_weights, select, labels)


def bulk_fluxes(air, sea):
    shear_u = air[2] - sea[2]
    shear_v = air[3] - sea[3]
    wind_speed = jnp.sqrt(shear_u * shear_u + shear_v * shear_v + 1.0)
    stress_u = 0.8 * wind_speed * shear_u
    stress_v = 0.8 * wind_speed * shear_v
    sensible = 0.6 * wind_speed * (sea[0] - air[0])
    saturated = 0.6 * jnp.exp(0.3 * sea[0]) * (1.0 - 0.1 * jnp.tanh(sea[1]))
    latent = 0.5 * wind_speed * (saturated - air[1])
    return (
        [sensible, latent, -stress_u, -stress_v],
        [-(sensible + latent), latent, stress_u, stress_v],
    )


def flux_kernel(fields, arrived_ref, grid_ref, answer_ref):
    devs, depth, _ = arrived_ref.shape
    per = fields * CAP
    arrived = arrived_ref[...].astype(F32)
    values = arrived[:, :per].reshape(devs * per, TILE).astype(BF16)
    labels = jnp.concatenate([arrived[:, per:]] * (per // 8), axis=1)
    field = lax.broadcasted_iota(jnp.int32, labels.shape, 1) // CAP
    codes = (labels + (field * (2 * XB_DEV)).astype(F32)).reshape(devs * per, TILE)
    codes = jnp.where(labels.reshape(devs * per, TILE) < 0.0, -1.0, codes)
    lane = lax.broadcasted_iota(jnp.int32, (1, TILE), 1)
    side, rest = lane // (fields * XB_DEV), lane % (fields * XB_DEV)
    code_of = side * XB_DEV + rest % XB_DEV + rest // XB_DEV * (2 * XB_DEV)
    hot = jnp.where(codes == code_of.astype(F32), 1.0, 0.0).astype(BF16)
    sums = lax.dot_general(hot, values, (((0,), (0,)), ((), ())), preferred_element_type=F32)
    rows = [sums[XB_DEV * k : XB_DEV * (k + 1)] for k in range(2 * fields)]
    atm_flux, ocn_flux = bulk_fluxes(rows[:fields], rows[fields:])
    table = jnp.concatenate(atm_flux + ocn_flux, axis=0).astype(BF16)
    to = lax.broadcasted_iota(jnp.int32, (TILE, TILE), 0)
    at = lax.broadcasted_iota(jnp.int32, (TILE, TILE), 1)
    both = 2 * fields
    moves = jnp.where(at == to % both * XB_DEV + to // both, 1.0, 0.0).astype(BF16)
    moved = jnp.dot(moves, table, preferred_element_type=F32)
    grid_ref[...] = moved.reshape(XB_DEV, both, TILE).astype(BF16)
    answer = jnp.dot(hot, table, preferred_element_type=F32)
    answer_ref[...] = answer.reshape(devs, per, TILE).astype(BF16)


def fluxes(arrived, fields):
    devs, _, _ = arrived.shape
    return pl.pallas_call(
        functools.partial(flux_kernel, fields),
        out_shape=(
            jax.ShapeDtypeStruct((XB_DEV, 2 * fields, TILE), BF16),
            jax.ShapeDtypeStruct((devs, fields * CAP, TILE), BF16),
        ),
        in_specs=[in_vmem()],
        out_specs=(in_vmem(),) * 2,
        compiler_params=limit(8),
        name="fluxes",
    )(arrived)


def merged(places, values):
    sums = []
    for k, value in enumerate(values):
        whole = value
        for j in range(k):
            whole = whole + jnp.where(places[j] == places[k], values[j], 0.0)
        sums.append(whole)
    return sums


def fill_operator(out, links, metric, cols, first_col, all_cols):
    edges = links.shape[0]
    lane = lax.broadcasted_iota(jnp.int32, (edges, TILE), 1)
    away = links[:, cols] - (first_col + lane)
    away = jnp.where(away > all_cols // 2, away - all_cols, away)
    away = jnp.where(away < -(all_cols // 2), away + all_cols, away)
    place = (away + lane).astype(F32)
    value = metric[:, cols]
    places = [jnp.broadcast_to(place[k : k + 1], (8, TILE)) for k in range(edges)]
    values = [jnp.broadcast_to(value[k : k + 1], (8, TILE)) for k in range(edges)]
    sums = merged(places, values)
    places = [jnp.concatenate([v, v], axis=0).astype(BF16) for v in places]
    sums = [jnp.concatenate([v, v], axis=0).astype(BF16) for v in sums]
    row = lax.broadcasted_iota(jnp.int32, (16, TILE), 0).astype(F32)
    for group in range((TILE + 2 * HALO) // 16):
        here = (row + float(16 * group - HALO)).astype(BF16)
        found = jnp.zeros((16, TILE), BF16)
        for k in range(edges):
            found = jnp.where(places[k] == here, sums[k], found)
        out[16 * group : 16 * (group + 1)] = found
    return 1.0 - step_size * jnp.sum(value, axis=0, keepdims=True)


def diffuse_kernel(
    all_cols, start_ref, atm_hbm, ocn_hbm, atm_links, ocn_links, atm_metric, ocn_metric, atm_out, ocn_out, ends_ref,
    atm_ref, ocn_ref, even_ref, odd_ref, wide_ref, op_ref, atm_new, ocn_new, in_sems, out_sems,
):
    levels, padded_rows, _ = atm_ref.shape
    fields, ocn_levels, columns = ocn_ref.shape
    pairs = columns // (2 * TILE)
    span = TILE + 2 * HALO

    def into(pair):
        rows = pl.ds(pl.multiple_of(8 * pair, 8), 8)
        lands = pl.ds(pl.multiple_of(8 * pair + 8, 8), 8)
        cols = pl.ds(pl.multiple_of(2 * TILE * pair, TILE), 2 * TILE)
        return [
            pltpu.make_async_copy(atm_hbm.at[:, rows, :], atm_ref.at[:, lands, :], in_sems.at[pair, 0]),
            pltpu.make_async_copy(ocn_hbm.at[:, :, cols], ocn_ref.at[:, :, cols], in_sems.at[pair, 1]),
        ]

    def out_of(pair):
        slot = lax.rem(pair, 2)
        rows = pl.ds(pl.multiple_of(8 * pair, 8), 8)
        cols = pl.ds(pl.multiple_of(2 * TILE * pair, TILE), 2 * TILE)
        return [
            pltpu.make_async_copy(atm_new.at[slot], atm_out.at[:, rows, :], out_sems.at[slot, 0]),
            pltpu.make_async_copy(ocn_new.at[slot], ocn_out.at[:, :, cols], out_sems.at[slot, 1]),
        ]

    for pair in range(pairs):
        for copy in into(pair):
            copy.start()
    atm_ref[:, :8, :] = jnp.zeros((levels, 8, TILE), F32)
    atm_ref[:, padded_rows - 8 :, :] = jnp.zeros((levels, 8, TILE), F32)
    wide_ref[:, :HALO] = jnp.zeros((fields * ocn_levels, HALO), BF16)
    wide_ref[:, HALO + columns :] = jnp.zeros((fields * ocn_levels, HALO), BF16)

    def narrow(pair):
        both = atm_ref[:, pl.ds(pl.multiple_of(8 * pair, 8), 16), :]
        odd_ref[pair] = both[:, 4:12].reshape(levels * 8, TILE).astype(BF16)
        even_ref[pair] = both[:, 8:].reshape(levels * 8, TILE).astype(BF16)
        cols = pl.ds(pl.multiple_of(2 * TILE * pair, TILE), 2 * TILE)
        lands = pl.ds(pl.multiple_of(2 * TILE * pair + HALO, TILE), 2 * TILE)
        stack = jnp.concatenate([ocn_ref[field, :, cols] for field in range(fields)], axis=0)
        wide_ref[:, lands] = stack.astype(BF16)

    for copy in into(0):
        copy.wait()
    narrow(0)
    top = lax.broadcasted_iota(jnp.int32, (8, TILE), 0) < fields

    def one_pair(pair, carry):
        @pl.when(pair + 1 < pairs)
        def _():
            for copy in into(pair + 1):
                copy.wait()
            narrow(pair + 1)

        @pl.when(pair + 1 == pairs)
        def _():
            both = atm_ref[:, pl.ds(8 * pairs, 16), :]
            odd_ref[pairs] = both[:, 4:12].reshape(levels * 8, TILE).astype(BF16)

        @pl.when(pair >= 2)
        def _():
            for copy in out_of(pair - 2):
                copy.wait()

        slot = lax.rem(pair, 2)
        keeps = []
        for half in range(2):
            block = 2 * pair + half
            first_col = start_ref[0] + block * TILE
            cols = pl.ds(pl.multiple_of(block * TILE, TILE), TILE)
            for which, (links, metric) in enumerate(((atm_links, atm_metric), (ocn_links, ocn_metric))):
                keeps.append(fill_operator(op_ref.at[which, half], links, metric, cols, first_col, all_cols))
        beside = jnp.dot(
            jnp.concatenate([odd_ref[pair], even_ref[pair], odd_ref[pair + 1]], axis=1),
            jnp.concatenate([op_ref[0, 0], op_ref[0, 1]], axis=1),
            preferred_element_type=F32,
        )
        keep = jnp.where(top, keeps[0], keeps[2])
        lands = pl.ds(pl.multiple_of(8 * pair + 8, 8), 8)
        for level in range(levels):
            rows = beside[8 * level : 8 * level + 8]
            atm_new[slot, level] = atm_ref[level, lands, :] * keep + step_size * jnp.where(
                top, rows[:, :TILE], rows[:, TILE:]
            )
        for half in range(2):
            at = pl.multiple_of(2 * TILE * pair + half * TILE, TILE)
            beside = jnp.dot(wide_ref[:, pl.ds(at, span)], op_ref[1, half], preferred_element_type=F32)
            for field in range(fields):
                ocn_new[slot, field, :, half * TILE : (half + 1) * TILE] = (
                    ocn_ref[field, :, pl.ds(at, TILE)] * keeps[1 + 2 * half]
                    + step_size * beside[field * ocn_levels : (field + 1) * ocn_levels]
                )
        for copy in out_of(pair):
            copy.start()

        @pl.when(pair == 0)
        def _():
            for which in range(2):
                ends_ref[0, which] = op_ref[which, 0, :HALO]

        @pl.when(pair + 1 == pairs)
        def _():
            for which in range(2):
                ends_ref[1, which] = op_ref[which, 1, HALO + TILE :]

        return carry

    lax.fori_loop(0, pairs, one_pair, 0)
    for pair in (pairs - 2, pairs - 1):
        for copy in out_of(pair):
            copy.wait()


def diffusion(start, all_cols, atm_rows, ocn_state, atm_links, ocn_links, atm_metric, ocn_metric):
    levels, count, _ = atm_rows.shape
    fields, ocn_levels, columns = ocn_state.shape
    pairs = columns // (2 * TILE)
    span = TILE + 2 * HALO
    return pl.pallas_call(
        functools.partial(diffuse_kernel, all_cols),
        out_shape=(
            pltpu.HBM(atm_rows.shape, F32),
            pltpu.HBM(ocn_state.shape, F32),
            jax.ShapeDtypeStruct((2, 2, HALO, TILE), BF16),
        ),
        in_specs=[in_smem(), in_hbm(), in_hbm()] + [in_vmem()] * 4,
        out_specs=(in_hbm(), in_hbm(), in_vmem()),
        scratch_shapes=[
            pltpu.VMEM((levels, count + 16, TILE), F32),
            pltpu.VMEM(ocn_state.shape, F32),
            pltpu.VMEM((pairs, levels * 8, TILE), BF16),
            pltpu.VMEM((pairs + 1, levels * 8, TILE), BF16),
            pltpu.VMEM((fields * ocn_levels, columns + 2 * HALO), BF16),
            pltpu.VMEM((2, 2, span, TILE), BF16),
            pltpu.VMEM((2, levels, 8, TILE), F32),
            pltpu.VMEM((2, fields, ocn_levels, 2 * TILE), F32),
            pltpu.SemaphoreType.DMA((pairs, 2)),
            pltpu.SemaphoreType.DMA((2, 2)),
        ],
        compiler_params=limit(24),
        name="diffusion",
    )(start, outside(atm_rows), outside(ocn_state), atm_links, ocn_links, atm_metric, ocn_metric)


def spread_kernel(
    blocks, source_ref, returned_ref, select_ref, weight_ref, left_ref, right_ref, ends_ref, atm_hbm, ocn_hbm, out_ref,
    atm_ref, ocn_ref, row_ref, sems,
):
    copies = [
        pltpu.make_async_copy(atm_hbm, atm_ref, sems.at[0]),
        pltpu.make_async_copy(ocn_hbm, ocn_ref, sems.at[1]),
    ]
    for copy in copies:
        copy.start()
    tiles = weight_ref.shape[0]
    both = out_ref.shape[1]
    devs, per, _ = returned_ref.shape
    stack = returned_ref[...].reshape(devs * per, TILE)
    row_ref[...] = jnp.dot(select_ref[...], stack, preferred_element_type=F32)
    out_ref[...] = jnp.zeros_like(out_ref)

    def one_tile(tile, carry):
        block = lax.rem(source_ref[tile], blocks)
        back = lax.dot_general(
            row_ref[pl.ds(pl.multiple_of(both * tile, both), both)].astype(BF16),
            weight_ref[tile],
            (((1,), (1,)), ((), ())),
            preferred_element_type=F32,
        )
        out_ref[block] += back
        return carry

    lax.fori_loop(0, tiles, one_tile, 0, unroll=True)
    for copy in copies:
        copy.wait()
    levels, atm_rows, _ = atm_ref.shape
    fields, ocn_levels, columns = ocn_ref.shape
    first = levels * fields
    for halo, end, row, col in ((left_ref, 0, 0, 0), (right_ref, 1, atm_rows - fields, columns - TILE)):
        atm = step_size * jnp.dot(halo[:first], ends_ref[end, 0], preferred_element_type=F32)
        ocn = step_size * jnp.dot(halo[first:], ends_ref[end, 1], preferred_element_type=F32)
        for level in range(levels):
            atm_ref[level, row : row + fields, :] += atm[level * fields : (level + 1) * fields]
        for field in range(fields):
            ocn_ref[field, :, col : col + TILE] += ocn[field * ocn_levels : (field + 1) * ocn_levels]


def spreading(returned, tile_source, tile_weights, select, left, right, ends, atm_base, ocn_base, blocks, fields):
    tiles = tile_weights.shape[0]
    return pl.pallas_call(
        functools.partial(spread_kernel, blocks),
        out_shape=(
            jax.ShapeDtypeStruct((blocks, 2 * fields, TILE), F32),
            pltpu.VMEM(atm_base.shape, F32),
            pltpu.VMEM(ocn_base.shape, F32),
        ),
        in_specs=[in_smem()] + [in_vmem()] * 6 + [in_hbm()] * 2,
        out_specs=(in_vmem(),) * 3,
        scratch_shapes=[pltpu.VMEM((tiles * 2 * fields, TILE), F32), pltpu.SemaphoreType.DMA((2,))],
        compiler_params=limit(8),
        name="spreading",
    )(tile_source, returned, select, tile_weights, left, right, ends, outside(atm_base), outside(ocn_base))


def update_kernel(
    chunks, atm_ref, ocn_ref, own_ref, other_ref, atm_w, ocn_w, atm_out, ocn_out, atm_new, ocn_new, sems
):
    levels, atm_rows, _ = atm_ref.shape
    fields, ocn_levels, columns = ocn_ref.shape
    per = atm_rows // 8 // chunks
    wide = columns // chunks

    def out_of(chunk):
        rows = pl.ds(pl.multiple_of(chunk * 8 * per, 8), 8 * per)
        cols = pl.ds(pl.multiple_of(chunk * wide, TILE), wide)
        return [
            pltpu.make_async_copy(atm_new.at[:, rows, :], atm_out.at[:, rows, :], sems.at[chunk, 0]),
            pltpu.make_async_copy(ocn_new.at[:, :, cols], ocn_out.at[:, :, cols], sems.at[chunk, 1]),
        ]

    def one_chunk(chunk, carry):
        for inner in range(per):
            pair = chunk * per + inner
            flux = [flux_gain * (own_ref[2 * pair + half] + other_ref[2 * pair + half]) for half in range(2)]
            gain = jnp.concatenate([flux[0][:fields], flux[1][:fields]], axis=0)
            rows = pl.ds(pl.multiple_of(8 * pair, 8), 8)
            for level in range(levels):
                atm_new[level, rows, :] = atm_ref[level, rows, :] + atm_w[level] * gain
            for half in range(2):
                cols = pl.ds(pl.multiple_of((2 * pair + half) * TILE, TILE), TILE)
                for field in range(fields):
                    ocn_new[field, :, cols] = (
                        ocn_ref[field, :, cols] + ocn_w[...] * flux[half][fields + field : fields + field + 1]
                    )
        for copy in out_of(chunk):
            copy.start()
        return carry

    lax.fori_loop(0, chunks, one_chunk, 0)
    for chunk in range(chunks):
        for copy in out_of(chunk):
            copy.wait()


def update(atm_base, ocn_base, own, other, atm_wide, ocn_wide):
    chunks = 8
    return pl.pallas_call(
        functools.partial(update_kernel, chunks),
        out_shape=(
            jax.ShapeDtypeStruct(atm_base.shape, F32),
            jax.ShapeDtypeStruct(ocn_base.shape, F32),
        ),
        in_specs=[in_vmem()] * 6,
        out_specs=(in_hbm(),) * 2,
        scratch_shapes=[
            pltpu.VMEM(atm_base.shape, F32),
            pltpu.VMEM(ocn_base.shape, F32),
            pltpu.SemaphoreType.DMA((chunks, 2)),
        ],
        compiler_params=limit(12),
        name="update",
    )(held(atm_base), held(ocn_base), own, other, atm_wide, ocn_wide)


def neighbours(head, tail, axis):
    count = lax.axis_size(axis)
    if count % 2:
        onward = [(i, (i + 1) % count) for i in range(count)]
        return lax.ppermute(tail, axis, onward), lax.ppermute(head, axis, [(j, i) for i, j in onward])
    odd = lax.rem(lax.axis_index(axis), 2) == 1
    inner = [(i, i ^ 1) for i in range(count)]
    outer = [(i, (i - 1 if i % 2 == 0 else i + 1) % count) for i in range(count)]
    over_inner = lax.ppermute(jnp.where(odd, head, tail), axis, inner)
    over_outer = lax.ppermute(jnp.where(odd, tail, head), axis, outer)
    return jnp.where(odd, over_inner, over_outer), jnp.where(odd, over_outer, over_inner)


def routes(tile_source, tile_target, owner_map, blocks, fields, dev_count):
    tiles = tile_source.shape[0]
    xblocks = owner_map.shape[0]
    per = fields * CAP
    matched = tile_target[:, None] == jnp.arange(xblocks, dtype=jnp.int32)[None, :]
    placed_at = jnp.sum(jnp.where(matched, owner_map[None, :], 0), axis=1)
    owner = placed_at // XB_DEV
    side = (tile_source >= blocks).astype(jnp.int32)
    segment = side * XB_DEV + placed_at % XB_DEV
    index = jnp.arange(tiles, dtype=jnp.int32)
    before = (index[None, :] < index[:, None]) & (owner[None, :] == owner[:, None])
    rank = jnp.sum(before.astype(jnp.int32), axis=1)
    slots = jnp.arange(dev_count * 8, dtype=jnp.int32)
    at_slot = (slots[:, None] // 8 == owner[None, :]) & (slots[:, None] % CAP == rank[None, :])
    label = jnp.sum(jnp.where(at_slot, segment[None, :] + 1, 0), axis=1) - 1
    labels = jnp.broadcast_to(label.astype(F32)[:, None], (dev_count * 8, TILE)).reshape(dev_count, 8, TILE)
    field = jnp.arange(fields, dtype=jnp.int32)
    goes = jnp.where(
        side[:, None, None] == jnp.arange(2, dtype=jnp.int32)[None, :, None],
        (owner * per + rank)[:, None, None] + field[None, None, :] * CAP,
        -1,
    ).reshape(tiles * 2 * fields)
    rows = jnp.arange(dev_count * per, dtype=jnp.int32)
    to_slots = (rows[:, None] == goes[None, :]).astype(BF16)
    to_tiles = (goes[:, None] == rows[None, :]).astype(BF16)
    return labels, to_slots, to_tiles


def shards(
    atm_state,
    ocn_state,
    atm_weights,
    ocn_weights,
    atm_metric,
    ocn_metric,
    atm_links,
    ocn_links,
    tile_weights,
    tile_source,
    tile_target,
    owner_map,
):
    comp_count = lax.axis_size("comp")
    dev_count = comp_count * lax.axis_size("lev")
    fields, _, columns = atm_state.shape
    blocks = columns // TILE
    swap = [(0, 1), (1, 0)]

    atm_rows = to_rows(atm_state)
    part, head, tail, atm_wide, ocn_wide = surface(atm_rows, ocn_state, atm_weights, ocn_weights)
    part_other = lax.ppermute(part, "lev", swap)
    labels, to_slots, to_tiles = routes(tile_source, tile_target, owner_map, blocks, fields, dev_count)
    outgoing = contributions(part, part_other, tile_source, tile_weights, to_slots, labels)
    start = (lax.axis_index("comp") * columns).astype(jnp.int32).reshape(1)
    outgoing, start = lax.optimization_barrier((outgoing, start))
    arrived = lax.all_to_all(outgoing, BOTH, split_axis=0, concat_axis=0, tiled=True)
    atm_base, ocn_base, ends = diffusion(
        start, columns * comp_count, atm_rows, ocn_state, atm_links, ocn_links, atm_metric, ocn_metric
    )
    arrived, atm_base, ocn_base, ends = lax.optimization_barrier((arrived, atm_base, ocn_base, ends))
    xgrid, answer = fluxes(arrived, fields)
    answer, head, tail = lax.optimization_barrier((answer, head, tail))
    returned = lax.all_to_all(answer, BOTH, split_axis=0, concat_axis=0, tiled=True)
    left, right = neighbours(head, tail, "comp")
    returned, left, right = lax.optimization_barrier((returned, left, right))
    spread, atm_base, ocn_base = spreading(
        returned, tile_source, tile_weights, to_tiles, left, right, ends, atm_base, ocn_base, blocks, fields
    )
    spread_other = lax.ppermute(spread, "lev", swap)
    atm_new, ocn_new = update(atm_base, ocn_base, spread, spread_other, atm_wide, ocn_wide)
    return (from_rows(atm_new, fields), ocn_new, xgrid)


def solution(mesh):
    placed = (
        P(None, "lev", ("grp", "comp")),
        P(None, "lev", ("grp", "comp")),
        P("lev"),
        P("lev"),
        P(None, "comp"),
        P(None, "comp"),
        P(None, "comp"),
        P(None, "comp"),
        P(("comp", "lev"), None, None),
        P(("comp", "lev")),
        P(("comp", "lev")),
        P(),
    )
    return jax.shard_map(
        shards,
        mesh=mesh,
        in_specs=placed,
        out_specs=(
            P(None, "lev", ("grp", "comp")),
            P(None, "lev", ("grp", "comp")),
            P(("grp", "comp", "lev"), None, None),
        ),
        check_vma=False,
    )
```

```python
import functools

import jax
import jax.numpy as jnp
from jax import lax
from jax.experimental import pallas as pl
from jax.experimental.pallas import tpu as pltpu
from jax.sharding import PartitionSpec as P

HALO = 128
CAP = 4
XB_DEV = 16
TILE = 128
step_size = 1.0
flux_gain = 10.0
BF16 = jnp.bfloat16
F32 = jnp.float32
BOTH = ("comp", "lev")


def in_vmem():
    return pl.BlockSpec(memory_space=pltpu.VMEM)


def in_smem():
    return pl.BlockSpec(memory_space=pltpu.SMEM)


def in_hbm():
    return pl.BlockSpec(memory_space=pl.ANY)


def held(array):
    return pltpu.with_memory_space_constraint(array, pltpu.VMEM)


def outside(array):
    return pltpu.with_memory_space_constraint(array, pltpu.HBM)


def limit(mib):
    return pltpu.CompilerParams(vmem_limit_bytes=mib * 1024 * 1024)


def to_rows(state):
    fields, levels, columns = state.shape
    blocks = columns // TILE
    split = state.transpose(1, 0, 2).reshape(levels, fields, blocks, TILE)
    return split.transpose(0, 2, 1, 3).reshape(levels, blocks * fields, TILE)


def from_rows(rows, fields):
    levels, count, _ = rows.shape
    blocks = count // fields
    split = rows.reshape(levels, blocks, fields, TILE).transpose(0, 2, 1, 3)
    return split.reshape(levels, fields, blocks * TILE).transpose(1, 0, 2)


def upper_half(fields):
    return lax.broadcasted_iota(jnp.int32, (8, TILE), 0) < fields


def turned(rows):
    return pltpu.roll(rows, 4, 0)


def halves(atm_ref, row, top):
    rows = [[], []]
    for level in range(0, atm_ref.shape[0], 2):
        low, high = atm_ref[level, pl.ds(row, 8), :], atm_ref[level + 1, pl.ds(row, 8), :]
        rows[0].append(jnp.where(top, low, turned(high)))
        rows[1].append(jnp.where(top, turned(low), high))
    return [jnp.concatenate(part, axis=0) for part in rows]


def over_lanes(values_ref, out_ref):
    for level in range(out_ref.shape[0]):
        out_ref[level : level + 1] = jnp.full((1, TILE), values_ref[level], F32)


def surface_kernel(
    chunks, paired, atm_hbm, ocn_hbm, atm_w, ocn_w, part_ref, inner_ref, outer_ref, atm_wide_hbm,
    ocn_wide_hbm, atm_ref, ocn_ref, ends_ref, atm_wide, ocn_wide, atm_s, ocn_s, sems, few_sems, wide_sems,
):
    levels, atm_rows, _ = atm_ref.shape
    fields, ocn_levels, columns = ocn_ref.shape
    deep = atm_rows // chunks
    wide = columns // chunks
    top = upper_half(fields)
    copies = []
    for chunk in range(chunks):
        rows = pl.ds(chunk * deep, deep)
        cols = pl.ds(chunk * wide, wide)
        for which, (src, dst) in enumerate(
            ((atm_hbm.at[:, rows, :], atm_ref.at[:, rows, :]), (ocn_hbm.at[:, :, cols], ocn_ref.at[:, :, cols]))
        ):
            copy = pltpu.make_async_copy(src, dst, sems.at[chunk, which])
            copy.start()
            copies.append(copy)
    few = [
        pltpu.make_async_copy(atm_w, atm_s, few_sems.at[0]),
        pltpu.make_async_copy(ocn_w, ocn_s, few_sems.at[1]),
    ]
    for copy in few:
        copy.start()
    for copy in few:
        copy.wait()
    over_lanes(atm_s, atm_wide)
    over_lanes(ocn_s, ocn_wide)
    wides = [
        pltpu.make_async_copy(atm_wide, atm_wide_hbm, wide_sems.at[0]),
        pltpu.make_async_copy(ocn_wide, ocn_wide_hbm, wide_sems.at[1]),
    ]
    for copy in wides:
        copy.start()
    for chunk in range(chunks):
        copies[2 * chunk].wait()
        copies[2 * chunk + 1].wait()

        def one_pair(pair, carry):
            rows = pl.ds(pl.multiple_of(pair * 8, 8), 8)
            atm = atm_ref[0, rows, :] * atm_wide[:1]
            for level in range(1, levels):
                atm = atm + atm_ref[level, rows, :] * atm_wide[level : level + 1]
            for half in range(2):
                block = 2 * pair + half
                cols = pl.ds(pl.multiple_of(block * TILE, TILE), TILE)
                ocn = [
                    jnp.sum(ocn_ref[field, :, cols] * ocn_wide[...], axis=0, keepdims=True) for field in range(fields)
                ]
                part_ref[block] = jnp.concatenate([atm[half * fields : (half + 1) * fields]] + ocn, axis=0)
            return carry

        lax.fori_loop(chunk * (deep // 8), (chunk + 1) * (deep // 8), one_pair, 0)
    ends_ref[0] = jnp.concatenate(
        [halves(atm_ref, 0, top)[0]] + [ocn_ref[field, :, :HALO] for field in range(fields)], axis=0
    ).astype(BF16)
    ends_ref[1] = jnp.concatenate(
        [halves(atm_ref, atm_rows - 8, top)[1]] + [ocn_ref[field, :, columns - HALO :] for field in range(fields)], axis=0
    ).astype(BF16)
    first_block = lax.rem(lax.axis_index("comp"), 2) if paired else 0
    inner_ref[...] = ends_ref[1 - first_block]
    outer_ref[...] = ends_ref[first_block]
    for copy in wides:
        copy.wait()


def surface(atm_rows, ocn_state, atm_weights, ocn_weights, paired):
    levels, count, _ = atm_rows.shape
    fields, ocn_levels, columns = ocn_state.shape
    rows = fields * (levels + ocn_levels)
    chunks = 4
    return pl.pallas_call(
        functools.partial(surface_kernel, chunks, paired),
        out_shape=(
            jax.ShapeDtypeStruct((columns // TILE, 2 * fields, TILE), F32),
            jax.ShapeDtypeStruct((rows, HALO), BF16),
            jax.ShapeDtypeStruct((rows, HALO), BF16),
            pltpu.HBM((levels, TILE), F32),
            pltpu.HBM((ocn_levels, TILE), F32),
        ),
        in_specs=[in_hbm()] * 4,
        out_specs=(in_vmem(),) * 3 + (in_hbm(),) * 2,
        scratch_shapes=[
            pltpu.VMEM(atm_rows.shape, F32),
            pltpu.VMEM(ocn_state.shape, F32),
            pltpu.VMEM((2, rows, HALO), BF16),
            pltpu.VMEM((levels, TILE), F32),
            pltpu.VMEM((ocn_levels, TILE), F32),
            pltpu.SMEM((levels,), F32),
            pltpu.SMEM((ocn_levels,), F32),
            pltpu.SemaphoreType.DMA((chunks, 2)),
            pltpu.SemaphoreType.DMA((2,)),
            pltpu.SemaphoreType.DMA((2,)),
        ],
        compiler_params=limit(12),
        name="surface",
    )(outside(atm_rows), outside(ocn_state), outside(atm_weights), outside(ocn_weights))


def contrib_kernel(
    blocks, source_ref, own_ref, other_ref, weight_ref, select_ref, label_ref, out_ref, surf_ref, row_ref
):
    surf_ref[...] = (own_ref[...] + other_ref[...]).astype(BF16).astype(F32)
    tiles = weight_ref.shape[0]
    both = own_ref.shape[1]
    devs, depth, _ = out_ref.shape

    for tile in range(tiles):
        block = lax.rem(source_ref[tile], blocks)
        row_ref[both * tile : both * (tile + 1)] = jnp.dot(
            surf_ref[block].astype(BF16), weight_ref[tile], preferred_element_type=F32
        )
    placed = jnp.dot(select_ref[...], row_ref[...].astype(BF16), preferred_element_type=F32)
    placed = placed.reshape(devs, depth - 8, TILE)
    out_ref[...] = jnp.concatenate([placed, label_ref[...]], axis=1).astype(BF16)


def contributions(own, other, tile_source, tile_weights, select, labels):
    blocks, both, _ = own.shape
    tiles = tile_weights.shape[0]
    devs = labels.shape[0]
    return pl.pallas_call(
        functools.partial(contrib_kernel, blocks),
        out_shape=jax.ShapeDtypeStruct((devs, CAP * both // 2 + 8, TILE), BF16),
        in_specs=[in_smem()] + [in_vmem()] * 5,
        out_specs=in_vmem(),
        scratch_shapes=[pltpu.VMEM(own.shape, F32), pltpu.VMEM((tiles * both, TILE), F32)],
        compiler_params=limit(8),
        name="contributions",
    )(tile_source, own, other, tile_weights, select, labels)


def bulk_fluxes(air, sea):
    shear_u = air[2] - sea[2]
    shear_v = air[3] - sea[3]
    wind_speed = jnp.sqrt(shear_u * shear_u + shear_v * shear_v + 1.0)
    stress_u = 0.8 * wind_speed * shear_u
    stress_v = 0.8 * wind_speed * shear_v
    sensible = 0.6 * wind_speed * (sea[0] - air[0])
    saturated = 0.6 * jnp.exp(0.3 * sea[0]) * (1.0 - 0.1 * jnp.tanh(sea[1]))
    latent = 0.5 * wind_speed * (saturated - air[1])
    return (
        [sensible, latent, -stress_u, -stress_v],
        [-(sensible + latent), latent, stress_u, stress_v],
    )


def flux_kernel(fields, arrived_ref, grid_ref, answer_ref):
    devs, depth, _ = arrived_ref.shape
    per = fields * CAP
    arrived = arrived_ref[...].astype(F32)
    values = arrived[:, :per].reshape(devs * per, TILE).astype(BF16)
    labels = jnp.concatenate([arrived[:, per:]] * (per // 8), axis=1)
    field = lax.broadcasted_iota(jnp.int32, labels.shape, 1) // CAP
    codes = (labels + (field * (2 * XB_DEV)).astype(F32)).reshape(devs * per, TILE)
    codes = jnp.where(labels.reshape(devs * per, TILE) < 0.0, -1.0, codes)
    lane = lax.broadcasted_iota(jnp.int32, (1, TILE), 1)
    side, rest = lane // (fields * XB_DEV), lane % (fields * XB_DEV)
    code_of = side * XB_DEV + rest % XB_DEV + rest // XB_DEV * (2 * XB_DEV)
    hot = jnp.where(codes == code_of.astype(F32), 1.0, 0.0).astype(BF16)
    sums = lax.dot_general(hot, values, (((0,), (0,)), ((), ())), preferred_element_type=F32)
    rows = [sums[XB_DEV * k : XB_DEV * (k + 1)] for k in range(2 * fields)]
    atm_flux, ocn_flux = bulk_fluxes(rows[:fields], rows[fields:])
    table = jnp.concatenate(atm_flux + ocn_flux, axis=0).astype(BF16)
    to = lax.broadcasted_iota(jnp.int32, (TILE, TILE), 0)
    at = lax.broadcasted_iota(jnp.int32, (TILE, TILE), 1)
    both = 2 * fields
    moves = jnp.where(at == to % both * XB_DEV + to // both, 1.0, 0.0).astype(BF16)
    moved = jnp.dot(moves, table, preferred_element_type=F32)
    grid_ref[...] = moved.reshape(XB_DEV, both, TILE).astype(BF16)
    answer = jnp.dot(hot, table, preferred_element_type=F32)
    answer_ref[...] = answer.reshape(devs, per, TILE).astype(BF16)


def fluxes(arrived, fields):
    devs, _, _ = arrived.shape
    return pl.pallas_call(
        functools.partial(flux_kernel, fields),
        out_shape=(
            jax.ShapeDtypeStruct((XB_DEV, 2 * fields, TILE), BF16),
            jax.ShapeDtypeStruct((devs, fields * CAP, TILE), BF16),
        ),
        in_specs=[in_vmem()],
        out_specs=(in_vmem(),) * 2,
        compiler_params=limit(8),
        name="fluxes",
    )(arrived)


def fill_operator(out, grid_ref, links, metric, cols, first_col, all_cols):
    edges = links.shape[0]
    lane = lax.broadcasted_iota(jnp.int32, (edges, TILE), 1)
    away = links[:, cols] - (first_col + lane)
    away = jnp.where(away > all_cols // 2, away - all_cols, away)
    away = jnp.where(away < -(all_cols // 2), away + all_cols, away)
    place = (away + lane).astype(F32)
    value = step_size * metric[:, cols]
    keep = 1.0 - jnp.sum(value, axis=0, keepdims=True)
    place = jnp.concatenate([place, jnp.full((8 - edges, TILE), -1.0e6, F32)], axis=0)
    value = jnp.concatenate([value, jnp.zeros((8 - edges, TILE), F32)], axis=0)
    edge = lax.broadcasted_iota(jnp.int32, (8, TILE), 0)
    whole = value
    for back in range(1, edges):
        same = (pltpu.roll(place, back, 0) == place) & (edge >= back)
        whole = whole + jnp.where(same, pltpu.roll(value, back, 0), 0.0)
    places = [jnp.broadcast_to(place[k : k + 1], (16, TILE)).astype(BF16) for k in range(edges)]
    sums = [jnp.broadcast_to(whole[k : k + 1], (16, TILE)).astype(BF16) for k in range(edges)]
    lanes = lax.broadcasted_iota(jnp.int32, (16, TILE), 1).astype(F32).astype(BF16)
    keep = jnp.broadcast_to(keep, (16, TILE)).astype(BF16)
    for group in range((TILE + 2 * HALO) // 16):
        here = grid_ref[16 * group : 16 * (group + 1)]
        found = jnp.zeros((16, TILE), BF16)
        if HALO <= 16 * group < HALO + TILE:
            found = jnp.where(lanes == here, keep, found)
        for k in range(edges):
            found = jnp.where(places[k] == here, sums[k], found)
        out[16 * group : 16 * (group + 1)] = found


def place_grid(grid_ref):
    grid_ref[...] = (lax.broadcasted_iota(jnp.int32, grid_ref.shape, 0) - HALO).astype(F32).astype(BF16)


def fill_pair(op, grid_ref, links, metric, pair, first_col, all_cols):
    span = TILE + 2 * HALO
    for half in range(2):
        at = (2 * pair + half) * TILE
        cols = pl.ds(pl.multiple_of(at, TILE), TILE)
        lanes = slice(half * TILE, (half + 1) * TILE)
        fill_operator(op.at[half * TILE : half * TILE + span, lanes], grid_ref, links, metric, cols, first_col + at, all_cols)


def clear_corners(op):
    op[TILE + 2 * HALO :, :TILE] = jnp.zeros((TILE, TILE), BF16)
    op[:TILE, TILE:] = jnp.zeros((TILE, TILE), BF16)


def edge_columns(inner_ref, outer_ref, rows, paired):
    inner, outer = inner_ref[rows], outer_ref[rows]
    if not paired:
        return inner, outer
    odd = lax.rem(lax.axis_index("comp"), 2) == 1
    return jnp.where(odd, inner, outer), jnp.where(odd, outer, inner)


def diffuse_kernel(
    all_cols, paired, atm_hbm, inner_ref, outer_ref, links, metric, base_hbm, edges_hbm, atm_ref, wide_ref, base_ref,
    edges_ref, even_op, odd_op, grid_ref, in_sems, out_sems, edge_sem,
):
    levels, atm_rows, _ = atm_ref.shape
    rows, columns = base_ref.shape
    pairs = columns // (2 * TILE)
    fields = rows // levels
    top = upper_half(fields)
    first_col = lax.axis_index("comp") * columns
    parts = in_sems.shape[0]
    deep = atm_rows // parts

    def into(index):
        at = pl.ds(deep * index, deep)
        return pltpu.make_async_copy(atm_hbm.at[:, at, :], atm_ref.at[:, at, :], in_sems.at[index])

    def out_of(index):
        cols = pl.ds(pl.multiple_of(4 * TILE * index, TILE), 4 * TILE)
        return pltpu.make_async_copy(base_ref.at[:, cols], base_hbm.at[:, cols], out_sems.at[index])

    for index in range(parts):
        into(index).start()
    edges_ref[0], edges_ref[1] = edge_columns(inner_ref, outer_ref, slice(rows, None), paired)
    edges = pltpu.make_async_copy(edges_ref, edges_hbm, edge_sem)
    edges.start()
    place_grid(grid_ref)
    for op in (even_op, odd_op):
        clear_corners(op)
    wide_ref[:, :HALO], wide_ref[:, HALO + columns :] = edge_columns(inner_ref, outer_ref, slice(0, rows), paired)

    def narrow(pair):
        lands = pl.ds(pl.multiple_of(pair * 2 * TILE + HALO, TILE), 2 * TILE)
        both = halves(atm_ref, pl.multiple_of(8 * pair, 8), top)
        wide_ref[:, lands] = jnp.concatenate(both, axis=1).astype(BF16)

    def step(pair, op, next_op, ahead):
        at = pl.multiple_of(pair * 2 * TILE, 2 * TILE)
        done = jnp.dot(wide_ref[:, pl.ds(at, 2 * TILE + 2 * HALO)], op[...], preferred_element_type=F32)
        if next_op is not None:
            fill_pair(next_op, grid_ref, links, metric, pair + 1, first_col, all_cols)
        if ahead:
            narrow(pair + 2)
        base_ref[:, pl.ds(at, 2 * TILE)] = done.astype(BF16)

    fill_pair(even_op, grid_ref, links, metric, 0, first_col, all_cols)
    into(0).wait()
    narrow(0)
    narrow(1)

    def two_pairs(index, carry):
        step(2 * index, even_op, odd_op, True)
        step(2 * index + 1, odd_op, even_op, True)
        out_of(index).start()
        return carry

    for part in range(parts):
        last = part == parts - 1
        if not last:
            into(part + 1).wait()
        per = pairs // 2 // parts
        lax.fori_loop(part * per, (part + 1) * per - last, two_pairs, 0)
    step(pairs - 2, even_op, odd_op, False)
    step(pairs - 1, odd_op, None, False)
    out_of(pairs // 2 - 1).start()
    for index in range(pairs // 2):
        out_of(index).wait()
    edges.wait()


def diffusion(all_cols, paired, atm_rows, inner, outer, links, metric):
    levels, count, _ = atm_rows.shape
    columns = links.shape[1]
    rows = levels * count // (columns // TILE)
    edges = (2, inner.shape[0] - rows, HALO)
    return pl.pallas_call(
        functools.partial(diffuse_kernel, all_cols, paired),
        out_shape=(pltpu.HBM((rows, columns), BF16), pltpu.HBM(edges, BF16)),
        in_specs=[in_hbm()] + [in_vmem()] * 4,
        out_specs=(in_hbm(),) * 2,
        scratch_shapes=[
            pltpu.VMEM(atm_rows.shape, F32),
            pltpu.VMEM((rows, columns + 2 * HALO), BF16),
            pltpu.VMEM((rows, columns), BF16),
            pltpu.VMEM(edges, BF16),
            pltpu.VMEM((2 * (TILE + HALO), 2 * TILE), BF16),
            pltpu.VMEM((2 * (TILE + HALO), 2 * TILE), BF16),
            pltpu.VMEM((TILE + 2 * HALO, TILE), BF16),
            pltpu.SemaphoreType.DMA((4,)),
            pltpu.SemaphoreType.DMA((columns // (4 * TILE),)),
            pltpu.SemaphoreType.DMA,
        ],
        compiler_params=limit(12),
        name="diffusion",
    )(outside(atm_rows), inner, outer, links, metric)


def spread_kernel(blocks, source_ref, returned_ref, select_ref, weight_ref, out_ref, row_ref):
    tiles = weight_ref.shape[0]
    both = out_ref.shape[1]
    devs, per, _ = returned_ref.shape
    stack = returned_ref[...].reshape(devs * per, TILE)
    row_ref[...] = jnp.dot(select_ref[...], stack, preferred_element_type=F32)
    out_ref[...] = jnp.zeros_like(out_ref)
    for tile in range(tiles):
        block = lax.rem(source_ref[tile], blocks)
        back = lax.dot_general(
            row_ref[both * tile : both * (tile + 1)].astype(BF16),
            weight_ref[tile],
            (((1,), (1,)), ((), ())),
            preferred_element_type=F32,
        )
        out_ref[block] += back


def spreading(returned, tile_source, tile_weights, select, blocks, fields):
    tiles = tile_weights.shape[0]
    return pl.pallas_call(
        functools.partial(spread_kernel, blocks),
        out_shape=jax.ShapeDtypeStruct((blocks, 2 * fields, TILE), F32),
        in_specs=[in_smem()] + [in_vmem()] * 3,
        out_specs=in_vmem(),
        scratch_shapes=[pltpu.VMEM((tiles * 2 * fields, TILE), F32)],
        compiler_params=limit(8),
        name="spreading",
    )(tile_source, returned, select, tile_weights)


def update_kernel(
    all_cols, atm_w, ocn_w, atm_base, ocn_hbm, edges_ref, ocn_links, ocn_metric, own_ref, other_ref,
    atm_out, ocn_out, ocn_wide, even_op, odd_op, grid_ref, ocn_ref, atm_new, ocn_new,
    in_sems, sems,
):
    levels, atm_rows, _ = atm_new.shape
    fields, ocn_levels, columns = ocn_ref.shape
    pairs = columns // (2 * TILE)
    top = upper_half(fields)
    comp = lax.axis_index("comp")

    def into(index):
        cols = pl.ds(pl.multiple_of(4 * TILE * index, TILE), 4 * TILE)
        return pltpu.make_async_copy(ocn_hbm.at[:, :, cols], ocn_ref.at[:, :, cols], in_sems.at[index])

    for index in range(pairs // 2):
        into(index).start()
    ocn_wide[:, :HALO] = edges_ref[0]
    ocn_wide[:, HALO + columns :] = edges_ref[1]
    for op in (even_op, odd_op):
        clear_corners(op)
    place_grid(grid_ref)

    def narrow(pair):
        at = pl.multiple_of(pair * 2 * TILE, 2 * TILE)
        lands = pl.ds(pl.multiple_of(at + HALO, TILE), 2 * TILE)
        ocn_wide[:, lands] = jnp.concatenate(
            [ocn_ref[field, :, pl.ds(at, 2 * TILE)] for field in range(fields)], axis=0
        ).astype(BF16)

    def fill(pair, op):
        fill_pair(op, grid_ref, ocn_links, ocn_metric, pair, comp * columns, all_cols)

    def gains(pair):
        return [flux_gain * (own_ref[2 * pair + half] + other_ref[2 * pair + half]) for half in range(2)]

    def atm_step(index):
        for pair in (2 * index, 2 * index + 1):
            flux = gains(pair)
            base = atm_base[:, pl.ds(pl.multiple_of(pair * 2 * TILE, 2 * TILE), 2 * TILE)].astype(F32)
            gain = jnp.concatenate([flux[0][:fields], flux[1][:fields]], axis=0)
            rows = pl.ds(pl.multiple_of(8 * pair, 8), 8)
            for level in range(0, levels, 2):
                here = base[level * fields : level * fields + 8]
                low = jnp.where(top, here[:, :TILE], turned(here[:, TILE:]))
                high = jnp.where(top, turned(here[:, :TILE]), here[:, TILE:])
                atm_new[level, rows, :] = low + atm_w[level : level + 1] * gain
                atm_new[level + 1, rows, :] = high + atm_w[level + 1 : level + 2] * gain
        atm_out_of(index).start()

    def ocn_step(pair, op, next_op, ahead):
        at = pl.multiple_of(pair * 2 * TILE, 2 * TILE)
        flux = gains(pair)
        done = jnp.dot(ocn_wide[:, pl.ds(at, 2 * TILE + 2 * HALO)], op[...], preferred_element_type=F32)
        if next_op is not None:
            fill(pair + 1, next_op)
        if ahead:
            narrow(pair + 2)
        for half in range(2):
            cols = pl.ds(pl.multiple_of(at + half * TILE, TILE), TILE)
            part = slice(half * TILE, (half + 1) * TILE)
            for field in range(fields):
                ocn_new[field, :, cols] = (
                    done[field * ocn_levels : (field + 1) * ocn_levels, part]
                    + ocn_w[...] * flux[half][fields + field : fields + field + 1]
                )

    def atm_out_of(index):
        rows = pl.ds(pl.multiple_of(16 * index, 16), 16)
        return pltpu.make_async_copy(atm_new.at[:, rows, :], atm_out.at[:, rows, :], sems.at[index, 0])

    def ocn_out_of(index):
        cols = pl.ds(pl.multiple_of(4 * TILE * index, TILE), 4 * TILE)
        return pltpu.make_async_copy(ocn_new.at[:, :, cols], ocn_out.at[:, :, cols], sems.at[index, 1])

    twos = pairs // 2
    lead = min(2, twos)
    for index in range(lead):
        atm_step(index)
    fill(0, even_op)
    into(0).wait()
    narrow(0)
    narrow(1)

    def two_pairs(index, carry):
        into(index + 1).wait()
        ocn_step(2 * index, even_op, odd_op, True)
        ocn_step(2 * index + 1, odd_op, even_op, True)
        ocn_out_of(index).start()

        @pl.when(index + lead < twos)
        def _():
            atm_step(index + lead)

        return carry

    lax.fori_loop(0, twos - 1, two_pairs, 0)
    ocn_step(pairs - 2, even_op, odd_op, False)
    ocn_step(pairs - 1, odd_op, None, False)
    ocn_out_of(twos - 1).start()
    for index in range(twos):
        atm_out_of(index).wait()
        ocn_out_of(index).wait()


def update(
    all_cols, atm_wide, ocn_wide, atm_base, ocn_state, edges, ocn_links, ocn_metric, own, other
):
    fields, ocn_levels, columns = ocn_state.shape
    atm_shape = (atm_wide.shape[0], columns // TILE * fields, TILE)
    return pl.pallas_call(
        functools.partial(update_kernel, all_cols),
        out_shape=(pltpu.HBM(atm_shape, F32), pltpu.HBM(ocn_state.shape, F32)),
        in_specs=[in_vmem()] * 3 + [in_hbm()] + [in_vmem()] * 5,
        out_specs=(in_hbm(),) * 2,
        scratch_shapes=[
            pltpu.VMEM((fields * ocn_levels, columns + 2 * HALO), BF16),
            pltpu.VMEM((2 * (TILE + HALO), 2 * TILE), BF16),
            pltpu.VMEM((2 * (TILE + HALO), 2 * TILE), BF16),
            pltpu.VMEM((TILE + 2 * HALO, TILE), BF16),
            pltpu.VMEM(ocn_state.shape, F32),
            pltpu.VMEM(atm_shape, F32),
            pltpu.VMEM(ocn_state.shape, F32),
            pltpu.SemaphoreType.DMA((columns // (4 * TILE),)),
            pltpu.SemaphoreType.DMA((columns // (4 * TILE), 2)),
        ],
        compiler_params=limit(20),
        name="update",
    )(atm_wide, ocn_wide, atm_base, outside(ocn_state), edges, ocn_links, ocn_metric, own, other)


def exchanged(inner, outer, axis):
    count = lax.axis_size(axis)
    if count % 2:
        onward = [(i, (i + 1) % count) for i in range(count)]
        return lax.ppermute(inner, axis, onward), lax.ppermute(outer, axis, [(j, i) for i, j in onward])
    within = [(i, i ^ 1) for i in range(count)]
    across = [(i, (i - 1 if i % 2 == 0 else i + 1) % count) for i in range(count)]
    return lax.ppermute(inner, axis, within), lax.ppermute(outer, axis, across)


def routes(tile_source, tile_target, owner_map, blocks, fields, dev_count):
    tiles = tile_source.shape[0]
    xblocks = owner_map.shape[0]
    per = fields * CAP
    matched = tile_target[:, None] == jnp.arange(xblocks, dtype=jnp.int32)[None, :]
    placed_at = jnp.sum(jnp.where(matched, owner_map[None, :], 0), axis=1)
    owner = placed_at // XB_DEV
    side = (tile_source >= blocks).astype(jnp.int32)
    segment = side * XB_DEV + placed_at % XB_DEV
    index = jnp.arange(tiles, dtype=jnp.int32)
    before = (index[None, :] < index[:, None]) & (owner[None, :] == owner[:, None])
    rank = jnp.sum(before.astype(jnp.int32), axis=1)
    slots = jnp.arange(dev_count * 8, dtype=jnp.int32)
    at_slot = (slots[:, None] // 8 == owner[None, :]) & (slots[:, None] % CAP == rank[None, :])
    label = jnp.sum(jnp.where(at_slot, segment[None, :] + 1, 0), axis=1) - 1
    labels = jnp.broadcast_to(label.astype(F32)[:, None], (dev_count * 8, TILE)).reshape(dev_count, 8, TILE)
    column = jnp.arange(tiles * 2 * fields, dtype=jnp.int32)
    mine = column[:, None] // (2 * fields) == index[None, :]
    packed = jnp.sum(jnp.where(mine, (2 * (owner * per + rank) + side)[None, :], 0), axis=1)
    goes = jnp.where(
        packed % 2 == column // fields % 2, packed // 2 + column % fields * CAP, -1
    )
    rows = jnp.arange(dev_count * per, dtype=jnp.int32)
    to_slots = (rows[:, None] == goes[None, :]).astype(BF16)
    to_tiles = (goes[:, None] == rows[None, :]).astype(BF16)
    return labels, to_slots, to_tiles


def shards(
    atm_state,
    ocn_state,
    atm_weights,
    ocn_weights,
    atm_metric,
    ocn_metric,
    atm_links,
    ocn_links,
    tile_weights,
    tile_source,
    tile_target,
    owner_map,
):
    comp_count = lax.axis_size("comp")
    dev_count = comp_count * lax.axis_size("lev")
    fields, _, columns = atm_state.shape
    blocks = columns // TILE
    swap = [(0, 1), (1, 0)]

    paired = comp_count % 2 == 0
    part, inner, outer, atm_wide, ocn_wide = surface(
        to_rows(atm_state), ocn_state, atm_weights, ocn_weights, paired
    )
    part_other = lax.ppermute(part, "lev", swap)
    labels, to_slots, to_tiles = routes(tile_source, tile_target, owner_map, blocks, fields, dev_count)
    outgoing = contributions(part, part_other, tile_source, tile_weights, to_slots, labels)
    outgoing, inner, outer = lax.optimization_barrier((outgoing, inner, outer))
    arrived = lax.all_to_all(outgoing, BOTH, split_axis=0, concat_axis=0, tiled=True)
    inner, outer = exchanged(inner, outer, "comp")
    xgrid, answer = fluxes(arrived, fields)
    answer, links = lax.optimization_barrier((answer, atm_links))
    returned = lax.all_to_all(answer, BOTH, split_axis=0, concat_axis=0, tiled=True)
    all_cols = columns * comp_count
    atm_base, edges = diffusion(all_cols, paired, to_rows(atm_state), inner, outer, links, atm_metric)
    returned, atm_base, edges = lax.optimization_barrier((returned, atm_base, edges))
    spread = spreading(returned, tile_source, tile_weights, to_tiles, blocks, fields)
    spread_other = lax.ppermute(spread, "lev", swap)
    atm_new, ocn_new = update(
        all_cols, atm_wide, ocn_wide, atm_base, ocn_state, edges, ocn_links, ocn_metric, spread, spread_other
    )
    return (from_rows(atm_new, fields), ocn_new, xgrid)


def solution(mesh):
    placed = (
        P(None, "lev", ("grp", "comp")),
        P(None, "lev", ("grp", "comp")),
        P("lev"),
        P("lev"),
        P(None, "comp"),
        P(None, "comp"),
        P(None, "comp"),
        P(None, "comp"),
        P(("comp", "lev"), None, None),
        P(("comp", "lev")),
        P(("comp", "lev")),
        P(),
    )
    return jax.shard_map(
        shards,
        mesh=mesh,
        in_specs=placed,
        out_specs=(
            P(None, "lev", ("grp", "comp")),
            P(None, "lev", ("grp", "comp")),
            P(("grp", "comp", "lev"), None, None),
        ),
        check_vma=False,
    )
```

```python
import functools

import jax
import jax.numpy as jnp
from jax import lax
from jax.experimental import pallas as pl
from jax.experimental.pallas import tpu as pltpu
from jax.sharding import PartitionSpec as P

HALO = 128
CAP = 4
XB_DEV = 16
TILE = 128
step_size = 1.0
flux_gain = 10.0
BF16 = jnp.bfloat16
F32 = jnp.float32
BOTH = ("comp", "lev")


def in_vmem():
    return pl.BlockSpec(memory_space=pltpu.VMEM)


def in_smem():
    return pl.BlockSpec(memory_space=pltpu.SMEM)


def in_hbm():
    return pl.BlockSpec(memory_space=pl.ANY)


def held(array):
    return pltpu.with_memory_space_constraint(array, pltpu.VMEM)


def outside(array):
    return pltpu.with_memory_space_constraint(array, pltpu.HBM)


def limit(mib):
    return pltpu.CompilerParams(vmem_limit_bytes=mib * 1024 * 1024)


def to_rows(state):
    fields, levels, columns = state.shape
    blocks = columns // TILE
    split = state.transpose(1, 0, 2).reshape(levels, fields, blocks, TILE)
    return split.transpose(0, 2, 1, 3).reshape(levels, blocks * fields, TILE)


def from_rows(rows, fields):
    levels, count, _ = rows.shape
    blocks = count // fields
    split = rows.reshape(levels, blocks, fields, TILE).transpose(0, 2, 1, 3)
    return split.reshape(levels, fields, blocks * TILE).transpose(1, 0, 2)


def upper_half(fields):
    return lax.broadcasted_iota(jnp.int32, (8, TILE), 0) < fields


def turned(rows):
    return pltpu.roll(rows, 4, 0)


def halves(atm_ref, row, top):
    rows = [[], []]
    for level in range(0, atm_ref.shape[0], 2):
        low, high = atm_ref[level, pl.ds(row, 8), :], atm_ref[level + 1, pl.ds(row, 8), :]
        rows[0].append(jnp.where(top, low, turned(high)))
        rows[1].append(jnp.where(top, turned(low), high))
    return [jnp.concatenate(part, axis=0) for part in rows]


def over_lanes(values_ref, out_ref):
    for level in range(out_ref.shape[0]):
        out_ref[level : level + 1] = jnp.full((1, TILE), values_ref[level], F32)


def surface_kernel(
    chunks, paired, atm_hbm, ocn_hbm, atm_w, ocn_w, part_ref, inner_ref, outer_ref, atm_wide_hbm,
    ocn_wide_hbm, atm_ref, ocn_ref, ends_ref, atm_wide, ocn_wide, atm_s, ocn_s, sems, few_sems, wide_sems,
):
    levels, atm_rows, _ = atm_ref.shape
    fields, ocn_levels, columns = ocn_ref.shape
    deep = atm_rows // chunks
    wide = columns // chunks
    top = upper_half(fields)
    copies = []
    for chunk in range(chunks):
        rows = pl.ds(chunk * deep, deep)
        cols = pl.ds(chunk * wide, wide)
        for which, (src, dst) in enumerate(
            ((atm_hbm.at[:, rows, :], atm_ref.at[:, rows, :]), (ocn_hbm.at[:, :, cols], ocn_ref.at[:, :, cols]))
        ):
            copy = pltpu.make_async_copy(src, dst, sems.at[chunk, which])
            copy.start()
            copies.append(copy)
    few = [
        pltpu.make_async_copy(atm_w, atm_s, few_sems.at[0]),
        pltpu.make_async_copy(ocn_w, ocn_s, few_sems.at[1]),
    ]
    for copy in few:
        copy.start()
    for copy in few:
        copy.wait()
    over_lanes(atm_s, atm_wide)
    over_lanes(ocn_s, ocn_wide)
    wides = [
        pltpu.make_async_copy(atm_wide, atm_wide_hbm, wide_sems.at[0]),
        pltpu.make_async_copy(ocn_wide, ocn_wide_hbm, wide_sems.at[1]),
    ]
    for copy in wides:
        copy.start()
    for chunk in range(chunks):
        copies[2 * chunk].wait()
        copies[2 * chunk + 1].wait()

        def one_pair(pair, carry):
            rows = pl.ds(pl.multiple_of(pair * 8, 8), 8)
            atm = atm_ref[0, rows, :] * atm_wide[:1]
            for level in range(1, levels):
                atm = atm + atm_ref[level, rows, :] * atm_wide[level : level + 1]
            for half in range(2):
                block = 2 * pair + half
                cols = pl.ds(pl.multiple_of(block * TILE, TILE), TILE)
                ocn = [
                    jnp.sum(ocn_ref[field, :, cols] * ocn_wide[...], axis=0, keepdims=True) for field in range(fields)
                ]
                part_ref[block] = jnp.concatenate([atm[half * fields : (half + 1) * fields]] + ocn, axis=0)
            return carry

        lax.fori_loop(chunk * (deep // 8), (chunk + 1) * (deep // 8), one_pair, 0)
    ends_ref[0] = jnp.concatenate(
        [halves(atm_ref, 0, top)[0]] + [ocn_ref[field, :, :HALO] for field in range(fields)], axis=0
    ).astype(BF16)
    ends_ref[1] = jnp.concatenate(
        [halves(atm_ref, atm_rows - 8, top)[1]] + [ocn_ref[field, :, columns - HALO :] for field in range(fields)], axis=0
    ).astype(BF16)
    first_block = lax.rem(lax.axis_index("comp"), 2) if paired else 0
    inner_ref[...] = ends_ref[1 - first_block]
    outer_ref[...] = ends_ref[first_block]
    for copy in wides:
        copy.wait()


def surface(atm_rows, ocn_state, atm_weights, ocn_weights, paired):
    levels, count, _ = atm_rows.shape
    fields, ocn_levels, columns = ocn_state.shape
    rows = fields * (levels + ocn_levels)
    chunks = 4
    return pl.pallas_call(
        functools.partial(surface_kernel, chunks, paired),
        out_shape=(
            jax.ShapeDtypeStruct((columns // TILE, 2 * fields, TILE), F32),
            jax.ShapeDtypeStruct((rows, HALO), BF16),
            jax.ShapeDtypeStruct((rows, HALO), BF16),
            pltpu.HBM((levels, TILE), F32),
            pltpu.HBM((ocn_levels, TILE), F32),
        ),
        in_specs=[in_hbm()] * 4,
        out_specs=(in_vmem(),) * 3 + (in_hbm(),) * 2,
        scratch_shapes=[
            pltpu.VMEM(atm_rows.shape, F32),
            pltpu.VMEM(ocn_state.shape, F32),
            pltpu.VMEM((2, rows, HALO), BF16),
            pltpu.VMEM((levels, TILE), F32),
            pltpu.VMEM((ocn_levels, TILE), F32),
            pltpu.SMEM((levels,), F32),
            pltpu.SMEM((ocn_levels,), F32),
            pltpu.SemaphoreType.DMA((chunks, 2)),
            pltpu.SemaphoreType.DMA((2,)),
            pltpu.SemaphoreType.DMA((2,)),
        ],
        compiler_params=limit(12),
        name="surface",
    )(outside(atm_rows), outside(ocn_state), outside(atm_weights), outside(ocn_weights))


def contrib_kernel(
    blocks, source_ref, own_ref, other_ref, weight_ref, select_ref, label_ref, out_ref, surf_ref, row_ref
):
    surf_ref[...] = (own_ref[...] + other_ref[...]).astype(BF16).astype(F32)
    tiles = weight_ref.shape[0]
    both = own_ref.shape[1]
    devs, depth, _ = out_ref.shape

    for tile in range(tiles):
        block = lax.rem(source_ref[tile], blocks)
        row_ref[both * tile : both * (tile + 1)] = jnp.dot(
            surf_ref[block].astype(BF16), weight_ref[tile], preferred_element_type=F32
        )
    placed = jnp.dot(select_ref[...], row_ref[...].astype(BF16), preferred_element_type=F32)
    placed = placed.reshape(devs, depth - 8, TILE)
    out_ref[...] = jnp.concatenate([placed, label_ref[...]], axis=1).astype(BF16)


def contributions(own, other, tile_source, tile_weights, select, labels):
    blocks, both, _ = own.shape
    tiles = tile_weights.shape[0]
    devs = labels.shape[0]
    return pl.pallas_call(
        functools.partial(contrib_kernel, blocks),
        out_shape=jax.ShapeDtypeStruct((devs, CAP * both // 2 + 8, TILE), BF16),
        in_specs=[in_smem()] + [in_vmem()] * 5,
        out_specs=in_vmem(),
        scratch_shapes=[pltpu.VMEM(own.shape, F32), pltpu.VMEM((tiles * both, TILE), F32)],
        compiler_params=limit(8),
        name="contributions",
    )(tile_source, own, other, tile_weights, select, labels)


def bulk_fluxes(air, sea):
    shear_u = air[2] - sea[2]
    shear_v = air[3] - sea[3]
    wind_speed = jnp.sqrt(shear_u * shear_u + shear_v * shear_v + 1.0)
    stress_u = 0.8 * wind_speed * shear_u
    stress_v = 0.8 * wind_speed * shear_v
    sensible = 0.6 * wind_speed * (sea[0] - air[0])
    saturated = 0.6 * jnp.exp(0.3 * sea[0]) * (1.0 - 0.1 * jnp.tanh(sea[1]))
    latent = 0.5 * wind_speed * (saturated - air[1])
    return (
        [sensible, latent, -stress_u, -stress_v],
        [-(sensible + latent), latent, stress_u, stress_v],
    )


def flux_kernel(fields, arrived_ref, grid_ref, answer_ref):
    devs, depth, _ = arrived_ref.shape
    per = fields * CAP
    arrived = arrived_ref[...].astype(F32)
    values = arrived[:, :per].reshape(devs * per, TILE).astype(BF16)
    labels = jnp.concatenate([arrived[:, per:]] * (per // 8), axis=1)
    field = lax.broadcasted_iota(jnp.int32, labels.shape, 1) // CAP
    codes = (labels + (field * (2 * XB_DEV)).astype(F32)).reshape(devs * per, TILE)
    codes = jnp.where(labels.reshape(devs * per, TILE) < 0.0, -1.0, codes)
    lane = lax.broadcasted_iota(jnp.int32, (1, TILE), 1)
    side, rest = lane // (fields * XB_DEV), lane % (fields * XB_DEV)
    code_of = side * XB_DEV + rest % XB_DEV + rest // XB_DEV * (2 * XB_DEV)
    hot = jnp.where(codes == code_of.astype(F32), 1.0, 0.0).astype(BF16)
    sums = lax.dot_general(hot, values, (((0,), (0,)), ((), ())), preferred_element_type=F32)
    rows = [sums[XB_DEV * k : XB_DEV * (k + 1)] for k in range(2 * fields)]
    atm_flux, ocn_flux = bulk_fluxes(rows[:fields], rows[fields:])
    table = jnp.concatenate(atm_flux + ocn_flux, axis=0).astype(BF16)
    to = lax.broadcasted_iota(jnp.int32, (TILE, TILE), 0)
    at = lax.broadcasted_iota(jnp.int32, (TILE, TILE), 1)
    both = 2 * fields
    moves = jnp.where(at == to % both * XB_DEV + to // both, 1.0, 0.0).astype(BF16)
    moved = jnp.dot(moves, table, preferred_element_type=F32)
    grid_ref[...] = moved.reshape(XB_DEV, both, TILE).astype(BF16)
    answer = jnp.dot(hot, table, preferred_element_type=F32)
    answer_ref[...] = answer.reshape(devs, per, TILE).astype(BF16)


def fluxes(arrived, fields):
    devs, _, _ = arrived.shape
    return pl.pallas_call(
        functools.partial(flux_kernel, fields),
        out_shape=(
            jax.ShapeDtypeStruct((XB_DEV, 2 * fields, TILE), BF16),
            jax.ShapeDtypeStruct((devs, fields * CAP, TILE), BF16),
        ),
        in_specs=[in_vmem()],
        out_specs=(in_vmem(),) * 2,
        compiler_params=limit(8),
        name="fluxes",
    )(arrived)


def fill_operator(out, grid_ref, links, metric, cols, first_col, all_cols):
    edges = links.shape[0]
    lane = lax.broadcasted_iota(jnp.int32, (edges, TILE), 1)
    away = links[:, cols] - (first_col + lane)
    away = jnp.where(away > all_cols // 2, away - all_cols, away)
    away = jnp.where(away < -(all_cols // 2), away + all_cols, away)
    place = (away + lane).astype(F32)
    value = step_size * metric[:, cols]
    keep = 1.0 - jnp.sum(value, axis=0, keepdims=True)
    place = jnp.concatenate([place, jnp.full((8 - edges, TILE), -1.0e6, F32)], axis=0)
    value = jnp.concatenate([value, jnp.zeros((8 - edges, TILE), F32)], axis=0)
    edge = lax.broadcasted_iota(jnp.int32, (8, TILE), 0)
    whole = value
    for back in range(1, edges):
        same = (pltpu.roll(place, back, 0) == place) & (edge >= back)
        whole = whole + jnp.where(same, pltpu.roll(value, back, 0), 0.0)
    places = [jnp.broadcast_to(place[k : k + 1], (16, TILE)).astype(BF16) for k in range(edges)]
    sums = [jnp.broadcast_to(whole[k : k + 1], (16, TILE)).astype(BF16) for k in range(edges)]
    lanes = lax.broadcasted_iota(jnp.int32, (16, TILE), 1).astype(F32).astype(BF16)
    keep = jnp.broadcast_to(keep, (16, TILE)).astype(BF16)
    for group in range((TILE + 2 * HALO) // 16):
        here = grid_ref[16 * group : 16 * (group + 1)]
        found = jnp.zeros((16, TILE), BF16)
        if HALO <= 16 * group < HALO + TILE:
            found = jnp.where(lanes == here, keep, found)
        for k in range(edges):
            found = jnp.where(places[k] == here, sums[k], found)
        out[16 * group : 16 * (group + 1)] = found


def place_grid(grid_ref):
    grid_ref[...] = (lax.broadcasted_iota(jnp.int32, grid_ref.shape, 0) - HALO).astype(F32).astype(BF16)


def fill_pair(op, grid_ref, links, metric, pair, first_col, all_cols):
    span = TILE + 2 * HALO
    for half in range(2):
        at = (2 * pair + half) * TILE
        cols = pl.ds(pl.multiple_of(at, TILE), TILE)
        lanes = slice(half * TILE, (half + 1) * TILE)
        fill_operator(op.at[half * TILE : half * TILE + span, lanes], grid_ref, links, metric, cols, first_col + at, all_cols)


def clear_corners(op):
    op[TILE + 2 * HALO :, :TILE] = jnp.zeros((TILE, TILE), BF16)
    op[:TILE, TILE:] = jnp.zeros((TILE, TILE), BF16)


def edge_columns(inner_ref, outer_ref, rows, paired):
    inner, outer = inner_ref[rows], outer_ref[rows]
    if not paired:
        return inner, outer
    odd = lax.rem(lax.axis_index("comp"), 2) == 1
    return jnp.where(odd, inner, outer), jnp.where(odd, outer, inner)


def diffuse_kernel(
    all_cols, paired, ocn_hbm, inner_ref, outer_ref, links, metric, base_hbm, edges_hbm, ocn_ref, wide_ref, base_ref,
    edges_ref, even_op, odd_op, grid_ref, in_sems, out_sems, edge_sem,
):
    fields, levels, columns = ocn_ref.shape
    rows = fields * levels
    first = inner_ref.shape[0] - rows
    pairs = columns // (2 * TILE)
    first_col = lax.axis_index("comp") * columns
    parts = in_sems.shape[0]
    wide_cols = columns // parts

    def into(index):
        cols = pl.ds(wide_cols * index, wide_cols)
        return pltpu.make_async_copy(ocn_hbm.at[:, :, cols], ocn_ref.at[:, :, cols], in_sems.at[index])

    def out_of(index):
        cols = pl.ds(pl.multiple_of(4 * TILE * index, TILE), 4 * TILE)
        return pltpu.make_async_copy(base_ref.at[:, cols], base_hbm.at[:, cols], out_sems.at[index])

    for index in range(parts):
        into(index).start()
    edges_ref[0], edges_ref[1] = edge_columns(inner_ref, outer_ref, slice(0, first), paired)
    edges = pltpu.make_async_copy(edges_ref, edges_hbm, edge_sem)
    edges.start()
    place_grid(grid_ref)
    for op in (even_op, odd_op):
        clear_corners(op)
    wide_ref[:, :HALO], wide_ref[:, HALO + columns :] = edge_columns(inner_ref, outer_ref, slice(first, None), paired)

    def narrow(pair):
        at = pl.multiple_of(pair * 2 * TILE, 2 * TILE)
        lands = pl.ds(pl.multiple_of(at + HALO, TILE), 2 * TILE)
        wide_ref[:, lands] = jnp.concatenate(
            [ocn_ref[field, :, pl.ds(at, 2 * TILE)] for field in range(fields)], axis=0
        ).astype(BF16)

    def step(pair, op, next_op, ahead):
        at = pl.multiple_of(pair * 2 * TILE, 2 * TILE)
        done = jnp.dot(wide_ref[:, pl.ds(at, 2 * TILE + 2 * HALO)], op[...], preferred_element_type=F32)
        if next_op is not None:
            fill_pair(next_op, grid_ref, links, metric, pair + 1, first_col, all_cols)
        if ahead:
            narrow(pair + 2)
        base_ref[:, pl.ds(at, 2 * TILE)] = done.astype(BF16)

    fill_pair(even_op, grid_ref, links, metric, 0, first_col, all_cols)
    into(0).wait()
    narrow(0)
    narrow(1)

    def two_pairs(index, carry):
        step(2 * index, even_op, odd_op, True)
        step(2 * index + 1, odd_op, even_op, True)
        out_of(index).start()
        return carry

    for part in range(parts):
        last = part == parts - 1
        if not last:
            into(part + 1).wait()
        per = pairs // 2 // parts
        lax.fori_loop(part * per, (part + 1) * per - last, two_pairs, 0)
    step(pairs - 2, even_op, odd_op, False)
    step(pairs - 1, odd_op, None, False)
    out_of(pairs // 2 - 1).start()
    for index in range(pairs // 2):
        out_of(index).wait()
    edges.wait()


def diffusion(all_cols, paired, ocn_state, inner, outer, links, metric):
    fields, levels, columns = ocn_state.shape
    rows = fields * levels
    edges = (2, inner.shape[0] - rows, HALO)
    return pl.pallas_call(
        functools.partial(diffuse_kernel, all_cols, paired),
        out_shape=(pltpu.HBM((rows, columns), BF16), pltpu.HBM(edges, BF16)),
        in_specs=[in_hbm()] + [in_vmem()] * 4,
        out_specs=(in_hbm(),) * 2,
        scratch_shapes=[
            pltpu.VMEM(ocn_state.shape, F32),
            pltpu.VMEM((rows, columns + 2 * HALO), BF16),
            pltpu.VMEM((rows, columns), BF16),
            pltpu.VMEM(edges, BF16),
            pltpu.VMEM((2 * (TILE + HALO), 2 * TILE), BF16),
            pltpu.VMEM((2 * (TILE + HALO), 2 * TILE), BF16),
            pltpu.VMEM((TILE + 2 * HALO, TILE), BF16),
            pltpu.SemaphoreType.DMA((4,)),
            pltpu.SemaphoreType.DMA((columns // (4 * TILE),)),
            pltpu.SemaphoreType.DMA,
        ],
        compiler_params=limit(12),
        name="diffusion",
    )(outside(ocn_state), inner, outer, links, metric)


def spread_kernel(blocks, source_ref, returned_ref, goes_ref, weight_ref, out_ref, row_ref):
    tiles = weight_ref.shape[0]
    both = out_ref.shape[1]
    devs, per, _ = returned_ref.shape
    stack = returned_ref[...].reshape(devs * per, TILE)
    rows = lax.broadcasted_iota(jnp.int32, (devs * per, goes_ref.shape[1]), 0)
    select = jnp.where(rows == goes_ref[...], 1.0, 0.0).astype(BF16)
    row_ref[...] = lax.dot_general(select, stack, (((0,), (0,)), ((), ())), preferred_element_type=F32)
    out_ref[...] = jnp.zeros_like(out_ref)
    for tile in range(tiles):
        block = lax.rem(source_ref[tile], blocks)
        back = lax.dot_general(
            row_ref[both * tile : both * (tile + 1)].astype(BF16),
            weight_ref[tile],
            (((1,), (1,)), ((), ())),
            preferred_element_type=F32,
        )
        out_ref[block] += back


def spreading(returned, tile_source, tile_weights, goes, blocks, fields):
    tiles = tile_weights.shape[0]
    return pl.pallas_call(
        functools.partial(spread_kernel, blocks),
        out_shape=jax.ShapeDtypeStruct((blocks, 2 * fields, TILE), F32),
        in_specs=[in_smem()] + [in_vmem()] * 3,
        out_specs=in_vmem(),
        scratch_shapes=[pltpu.VMEM((tiles * 2 * fields, TILE), F32)],
        compiler_params=limit(8),
        name="spreading",
    )(tile_source, returned, goes, tile_weights)


def update_kernel(
    all_cols, atm_w_hbm, ocn_w_hbm, ocn_base, atm_hbm, edges_hbm, links_hbm, metric_hbm, own_ref, other_ref, atm_out,
    ocn_out, atm_w, ocn_w, edges_ref, links, metric, wide_ref,
    even_op, odd_op, grid_ref, atm_ref, atm_new, ocn_new, few_sems, in_sems, sems,
):
    levels, _, _ = atm_new.shape
    fields, ocn_levels, columns = ocn_new.shape
    pairs = columns // (2 * TILE)
    twos = pairs // 2
    top = upper_half(fields)
    first_col = lax.axis_index("comp") * columns

    def into(index):
        rows = pl.ds(pl.multiple_of(16 * index, 16), 16)
        return pltpu.make_async_copy(atm_hbm.at[:, rows, :], atm_ref.at[:, rows, :], in_sems.at[index])

    def atm_out_of(index):
        rows = pl.ds(pl.multiple_of(16 * index, 16), 16)
        return pltpu.make_async_copy(atm_new.at[:, rows, :], atm_out.at[:, rows, :], sems.at[index, 0])

    def ocn_out_of(index):
        cols = pl.ds(pl.multiple_of(4 * TILE * index, TILE), 4 * TILE)
        return pltpu.make_async_copy(ocn_new.at[:, :, cols], ocn_out.at[:, :, cols], sems.at[index, 1])

    few = [
        pltpu.make_async_copy(src, dst, few_sems.at[k])
        for k, (src, dst) in enumerate(
            (
                (atm_w_hbm, atm_w),
                (ocn_w_hbm, ocn_w),
                (links_hbm, links),
                (metric_hbm, metric),
                (edges_hbm, edges_ref),
            )
        )
    ]
    for copy in few:
        copy.start()
    for index in range(twos):
        into(index).start()
    for op in (even_op, odd_op):
        clear_corners(op)
    place_grid(grid_ref)

    def narrow(pair):
        lands = pl.ds(pl.multiple_of(pair * 2 * TILE + HALO, TILE), 2 * TILE)
        both = halves(atm_ref, pl.multiple_of(8 * pair, 8), top)
        wide_ref[:, lands] = jnp.concatenate(both, axis=1).astype(BF16)

    def gains(pair):
        return [flux_gain * (own_ref[2 * pair + half] + other_ref[2 * pair + half]) for half in range(2)]

    def ocn_step(index):
        for pair in (2 * index, 2 * index + 1):
            flux = gains(pair)
            for half in range(2):
                cols = pl.ds(pl.multiple_of((2 * pair + half) * TILE, TILE), TILE)
                base = ocn_base[:, cols].astype(F32)
                for field in range(fields):
                    ocn_new[field, :, cols] = (
                        base[field * ocn_levels : (field + 1) * ocn_levels]
                        + ocn_w[...] * flux[half][fields + field : fields + field + 1]
                    )
        ocn_out_of(index).start()

    def atm_step(pair, op, next_op, ahead):
        at = pl.multiple_of(pair * 2 * TILE, 2 * TILE)
        flux = gains(pair)
        done = jnp.dot(wide_ref[:, pl.ds(at, 2 * TILE + 2 * HALO)], op[...], preferred_element_type=F32)
        if next_op is not None:
            fill_pair(next_op, grid_ref, links, metric, pair + 1, first_col, all_cols)
        if ahead:
            narrow(pair + 2)
        gain = jnp.concatenate([flux[0][:fields], flux[1][:fields]], axis=0)
        rows = pl.ds(pl.multiple_of(8 * pair, 8), 8)
        for level in range(0, levels, 2):
            here = done[level * fields : level * fields + 8]
            low = jnp.where(top, here[:, :TILE], turned(here[:, TILE:]))
            high = jnp.where(top, turned(here[:, :TILE]), here[:, TILE:])
            atm_new[level, rows, :] = low + atm_w[level : level + 1] * gain
            atm_new[level + 1, rows, :] = high + atm_w[level + 1 : level + 2] * gain

    lead = min(2, twos)
    for copy in few:
        copy.wait()
    for index in range(lead):
        ocn_step(index)
    wide_ref[:, :HALO] = edges_ref[0]
    wide_ref[:, HALO + columns :] = edges_ref[1]
    fill_pair(even_op, grid_ref, links, metric, 0, first_col, all_cols)
    into(0).wait()
    narrow(0)
    narrow(1)

    def two_pairs(index, carry):
        into(index + 1).wait()
        atm_step(2 * index, even_op, odd_op, True)
        atm_step(2 * index + 1, odd_op, even_op, True)
        atm_out_of(index).start()

        @pl.when(index + lead < twos)
        def _():
            ocn_step(index + lead)

        return carry

    lax.fori_loop(0, twos - 1, two_pairs, 0)
    atm_step(pairs - 2, even_op, odd_op, False)
    atm_step(pairs - 1, odd_op, None, False)
    atm_out_of(twos - 1).start()
    for index in range(twos):
        atm_out_of(index).wait()
        ocn_out_of(index).wait()


def update(all_cols, atm_wide, ocn_wide, ocn_base, atm_rows, edges, links, metric, own, other):
    levels, count, _ = atm_rows.shape
    ocn_levels, columns = ocn_wide.shape[0], links.shape[1]
    fields = own.shape[1] // 2
    ocn_shape = (fields, ocn_levels, columns)
    return pl.pallas_call(
        functools.partial(update_kernel, all_cols),
        out_shape=(pltpu.HBM(atm_rows.shape, F32), pltpu.HBM(ocn_shape, F32)),
        in_specs=[in_hbm()] * 2 + [in_vmem()] + [in_hbm()] * 4 + [in_vmem()] * 2,
        out_specs=(in_hbm(),) * 2,
        scratch_shapes=[
            pltpu.VMEM(atm_wide.shape, F32),
            pltpu.VMEM(ocn_wide.shape, F32),
            pltpu.VMEM(edges.shape, BF16),
            pltpu.VMEM(links.shape, links.dtype),
            pltpu.VMEM(metric.shape, F32),
            pltpu.VMEM((fields * levels, columns + 2 * HALO), BF16),
            pltpu.VMEM((2 * (TILE + HALO), 2 * TILE), BF16),
            pltpu.VMEM((2 * (TILE + HALO), 2 * TILE), BF16),
            pltpu.VMEM((TILE + 2 * HALO, TILE), BF16),
            pltpu.VMEM(atm_rows.shape, F32),
            pltpu.VMEM(atm_rows.shape, F32),
            pltpu.VMEM(ocn_shape, F32),
            pltpu.SemaphoreType.DMA((5,)),
            pltpu.SemaphoreType.DMA((columns // (4 * TILE),)),
            pltpu.SemaphoreType.DMA((columns // (4 * TILE), 2)),
        ],
        compiler_params=limit(20),
        name="update",
    )(
        outside(atm_wide), outside(ocn_wide), ocn_base, outside(atm_rows), outside(edges), outside(links),
        outside(metric), own, other,
    )


def exchanged(inner, outer, axis):
    count = lax.axis_size(axis)
    if count % 2:
        onward = [(i, (i + 1) % count) for i in range(count)]
        return lax.ppermute(inner, axis, onward), lax.ppermute(outer, axis, [(j, i) for i, j in onward])
    within = [(i, i ^ 1) for i in range(count)]
    across = [(i, (i - 1 if i % 2 == 0 else i + 1) % count) for i in range(count)]
    return lax.ppermute(inner, axis, within), lax.ppermute(outer, axis, across)


def routes(tile_source, tile_target, owner_map, blocks, fields, dev_count):
    tiles = tile_source.shape[0]
    xblocks = owner_map.shape[0]
    per = fields * CAP
    matched = tile_target[:, None] == jnp.arange(xblocks, dtype=jnp.int32)[None, :]
    placed_at = jnp.sum(jnp.where(matched, owner_map[None, :], 0), axis=1)
    owner = placed_at // XB_DEV
    side = (tile_source >= blocks).astype(jnp.int32)
    segment = side * XB_DEV + placed_at % XB_DEV
    index = jnp.arange(tiles, dtype=jnp.int32)
    before = (index[None, :] < index[:, None]) & (owner[None, :] == owner[:, None])
    rank = jnp.sum(before.astype(jnp.int32), axis=1)
    slots = jnp.arange(dev_count * 8, dtype=jnp.int32)
    at_slot = (slots[:, None] // 8 == owner[None, :]) & (slots[:, None] % CAP == rank[None, :])
    label = jnp.sum(jnp.where(at_slot, segment[None, :] + 1, 0), axis=1) - 1
    labels = jnp.broadcast_to(label.astype(F32)[:, None], (dev_count * 8, TILE)).reshape(dev_count, 8, TILE)
    column = jnp.arange(tiles * 2 * fields, dtype=jnp.int32)
    mine = column[:, None] // (2 * fields) == index[None, :]
    packed = jnp.sum(jnp.where(mine, (2 * (owner * per + rank) + side)[None, :], 0), axis=1)
    goes = jnp.where(
        packed % 2 == column // fields % 2, packed // 2 + column % fields * CAP, -1
    )
    rows = jnp.arange(dev_count * per, dtype=jnp.int32)
    to_slots = (rows[:, None] == goes[None, :]).astype(BF16)
    return labels, to_slots, goes[None, :]


def shards(
    atm_state,
    ocn_state,
    atm_weights,
    ocn_weights,
    atm_metric,
    ocn_metric,
    atm_links,
    ocn_links,
    tile_weights,
    tile_source,
    tile_target,
    owner_map,
):
    comp_count = lax.axis_size("comp")
    dev_count = comp_count * lax.axis_size("lev")
    fields, _, columns = atm_state.shape
    blocks = columns // TILE
    swap = [(0, 1), (1, 0)]

    paired = comp_count % 2 == 0
    part, inner, outer, atm_wide, ocn_wide = surface(
        to_rows(atm_state), ocn_state, atm_weights, ocn_weights, paired
    )
    part_other = lax.ppermute(part, "lev", swap)
    labels, to_slots, goes = routes(tile_source, tile_target, owner_map, blocks, fields, dev_count)
    outgoing = contributions(part, part_other, tile_source, tile_weights, to_slots, labels)
    outgoing, inner, outer = lax.optimization_barrier((outgoing, inner, outer))
    arrived = lax.all_to_all(outgoing, BOTH, split_axis=0, concat_axis=0, tiled=True)
    inner, outer = exchanged(inner, outer, "comp")
    xgrid, answer = fluxes(arrived, fields)
    answer, links = lax.optimization_barrier((answer, ocn_links))
    returned = lax.all_to_all(answer, BOTH, split_axis=0, concat_axis=0, tiled=True)
    all_cols = columns * comp_count
    ocn_base, edges = diffusion(all_cols, paired, ocn_state, inner, outer, links, ocn_metric)
    returned, ocn_base, edges = lax.optimization_barrier((returned, ocn_base, edges))
    spread = spreading(returned, tile_source, tile_weights, goes, blocks, fields)
    spread_other = lax.ppermute(spread, "lev", swap)
    atm_new, ocn_new = update(
        all_cols, atm_wide, ocn_wide, ocn_base, to_rows(atm_state), edges, atm_links, atm_metric, spread, spread_other
    )
    return (from_rows(atm_new, fields), ocn_new, xgrid)


def solution(mesh):
    placed = (
        P(None, "lev", ("grp", "comp")),
        P(None, "lev", ("grp", "comp")),
        P("lev"),
        P("lev"),
        P(None, "comp"),
        P(None, "comp"),
        P(None, "comp"),
        P(None, "comp"),
        P(("comp", "lev"), None, None),
        P(("comp", "lev")),
        P(("comp", "lev")),
        P(),
    )
    return jax.shard_map(
        shards,
        mesh=mesh,
        in_specs=placed,
        out_specs=(
            P(None, "lev", ("grp", "comp")),
            P(None, "lev", ("grp", "comp")),
            P(("grp", "comp", "lev"), None, None),
        ),
        check_vma=False,
    )
```

```python
import functools

import jax
import jax.numpy as jnp
from jax import lax
from jax.experimental import pallas as pl
from jax.experimental.pallas import tpu as pltpu
from jax.sharding import PartitionSpec as P

HALO = 128
CAP = 4
XB_DEV = 16
TILE = 128
step_size = 1.0
flux_gain = 10.0
BF16 = jnp.bfloat16
F32 = jnp.float32
BOTH = ("comp", "lev")


def in_vmem():
    return pl.BlockSpec(memory_space=pltpu.VMEM)


def in_smem():
    return pl.BlockSpec(memory_space=pltpu.SMEM)


def in_hbm():
    return pl.BlockSpec(memory_space=pl.ANY)


def held(array):
    return pltpu.with_memory_space_constraint(array, pltpu.VMEM)


def outside(array):
    return pltpu.with_memory_space_constraint(array, pltpu.HBM)


def limit(mib):
    return pltpu.CompilerParams(vmem_limit_bytes=mib * 1024 * 1024)


def to_rows(state):
    fields, levels, columns = state.shape
    blocks = columns // TILE
    split = state.transpose(1, 0, 2).reshape(levels, fields, blocks, TILE)
    return split.transpose(0, 2, 1, 3).reshape(levels, blocks * fields, TILE)


def from_rows(rows, fields):
    levels, count, _ = rows.shape
    blocks = count // fields
    split = rows.reshape(levels, blocks, fields, TILE).transpose(0, 2, 1, 3)
    return split.reshape(levels, fields, blocks * TILE).transpose(1, 0, 2)


def upper_half(fields):
    return lax.broadcasted_iota(jnp.int32, (8, TILE), 0) < fields


def turned(rows):
    return pltpu.roll(rows, 4, 0)


def halves(atm_ref, row, top):
    rows = [[], []]
    for level in range(0, atm_ref.shape[0], 2):
        low, high = atm_ref[level, pl.ds(row, 8), :], atm_ref[level + 1, pl.ds(row, 8), :]
        rows[0].append(jnp.where(top, low, turned(high)))
        rows[1].append(jnp.where(top, turned(low), high))
    return [jnp.concatenate(part, axis=0) for part in rows]


def over_lanes(values_ref, out_ref):
    for level in range(out_ref.shape[0]):
        out_ref[level : level + 1] = jnp.full((1, TILE), values_ref[level], F32)


def surface_kernel(
    chunks, paired, atm_hbm, ocn_hbm, atm_w, ocn_w, part_ref, inner_ref, outer_ref, atm_wide_hbm,
    ocn_wide_hbm, atm_ref, ocn_ref, ends_ref, atm_wide, ocn_wide, atm_s, ocn_s, sems, few_sems, wide_sems,
):
    levels, atm_rows, _ = atm_ref.shape
    fields, ocn_levels, columns = ocn_ref.shape
    deep = atm_rows // chunks
    wide = columns // chunks
    top = upper_half(fields)
    copies = []
    for chunk in range(chunks):
        rows = pl.ds(chunk * deep, deep)
        cols = pl.ds(chunk * wide, wide)
        for which, (src, dst) in enumerate(
            ((atm_hbm.at[:, rows, :], atm_ref.at[:, rows, :]), (ocn_hbm.at[:, :, cols], ocn_ref.at[:, :, cols]))
        ):
            copy = pltpu.make_async_copy(src, dst, sems.at[chunk, which])
            copy.start()
            copies.append(copy)
    few = [
        pltpu.make_async_copy(atm_w, atm_s, few_sems.at[0]),
        pltpu.make_async_copy(ocn_w, ocn_s, few_sems.at[1]),
    ]
    for copy in few:
        copy.start()
    for copy in few:
        copy.wait()
    over_lanes(atm_s, atm_wide)
    over_lanes(ocn_s, ocn_wide)
    wides = [
        pltpu.make_async_copy(atm_wide, atm_wide_hbm, wide_sems.at[0]),
        pltpu.make_async_copy(ocn_wide, ocn_wide_hbm, wide_sems.at[1]),
    ]
    for copy in wides:
        copy.start()
    for chunk in range(chunks):
        copies[2 * chunk].wait()
        copies[2 * chunk + 1].wait()

        def one_pair(pair, carry):
            rows = pl.ds(pl.multiple_of(pair * 8, 8), 8)
            atm = atm_ref[0, rows, :] * atm_wide[:1]
            for level in range(1, levels):
                atm = atm + atm_ref[level, rows, :] * atm_wide[level : level + 1]
            for half in range(2):
                block = 2 * pair + half
                cols = pl.ds(pl.multiple_of(block * TILE, TILE), TILE)
                ocn = [
                    jnp.sum(ocn_ref[field, :, cols] * ocn_wide[...], axis=0, keepdims=True) for field in range(fields)
                ]
                part_ref[block] = jnp.concatenate([atm[half * fields : (half + 1) * fields]] + ocn, axis=0)
            return carry

        lax.fori_loop(chunk * (deep // 8), (chunk + 1) * (deep // 8), one_pair, 0)
    ends_ref[0] = jnp.concatenate(
        [halves(atm_ref, 0, top)[0]] + [ocn_ref[field, :, :HALO] for field in range(fields)], axis=0
    ).astype(BF16)
    ends_ref[1] = jnp.concatenate(
        [halves(atm_ref, atm_rows - 8, top)[1]] + [ocn_ref[field, :, columns - HALO :] for field in range(fields)], axis=0
    ).astype(BF16)
    first_block = lax.rem(lax.axis_index("comp"), 2) if paired else 0
    inner_ref[...] = ends_ref[1 - first_block]
    outer_ref[...] = ends_ref[first_block]
    for copy in wides:
        copy.wait()


def surface(atm_rows, ocn_state, atm_weights, ocn_weights, paired):
    levels, count, _ = atm_rows.shape
    fields, ocn_levels, columns = ocn_state.shape
    rows = fields * (levels + ocn_levels)
    chunks = 8
    return pl.pallas_call(
        functools.partial(surface_kernel, chunks, paired),
        out_shape=(
            jax.ShapeDtypeStruct((columns // TILE, 2 * fields, TILE), F32),
            jax.ShapeDtypeStruct((rows, HALO), BF16),
            jax.ShapeDtypeStruct((rows, HALO), BF16),
            pltpu.HBM((levels, TILE), F32),
            pltpu.HBM((ocn_levels, TILE), F32),
        ),
        in_specs=[in_hbm()] * 4,
        out_specs=(in_vmem(),) * 3 + (in_hbm(),) * 2,
        scratch_shapes=[
            pltpu.VMEM(atm_rows.shape, F32),
            pltpu.VMEM(ocn_state.shape, F32),
            pltpu.VMEM((2, rows, HALO), BF16),
            pltpu.VMEM((levels, TILE), F32),
            pltpu.VMEM((ocn_levels, TILE), F32),
            pltpu.SMEM((levels,), F32),
            pltpu.SMEM((ocn_levels,), F32),
            pltpu.SemaphoreType.DMA((chunks, 2)),
            pltpu.SemaphoreType.DMA((2,)),
            pltpu.SemaphoreType.DMA((2,)),
        ],
        compiler_params=limit(12),
        name="surface",
    )(outside(atm_rows), outside(ocn_state), outside(atm_weights), outside(ocn_weights))


def contrib_kernel(
    blocks, source_ref, own_ref, other_ref, weight_ref, select_ref, label_ref, out_ref, surf_ref, row_ref
):
    surf_ref[...] = (own_ref[...] + other_ref[...]).astype(BF16).astype(F32)
    tiles = weight_ref.shape[0]
    both = own_ref.shape[1]
    devs, depth, _ = out_ref.shape

    for tile in range(tiles):
        block = lax.rem(source_ref[tile], blocks)
        row_ref[both * tile : both * (tile + 1)] = jnp.dot(
            surf_ref[block].astype(BF16), weight_ref[tile], preferred_element_type=F32
        )
    placed = jnp.dot(select_ref[...], row_ref[...].astype(BF16), preferred_element_type=F32)
    placed = placed.reshape(devs, depth - 8, TILE)
    out_ref[...] = jnp.concatenate([placed, label_ref[...]], axis=1).astype(BF16)


def contributions(own, other, tile_source, tile_weights, select, labels):
    blocks, both, _ = own.shape
    tiles = tile_weights.shape[0]
    devs = labels.shape[0]
    return pl.pallas_call(
        functools.partial(contrib_kernel, blocks),
        out_shape=jax.ShapeDtypeStruct((devs, CAP * both // 2 + 8, TILE), BF16),
        in_specs=[in_smem()] + [in_vmem()] * 5,
        out_specs=in_vmem(),
        scratch_shapes=[pltpu.VMEM(own.shape, F32), pltpu.VMEM((tiles * both, TILE), F32)],
        compiler_params=limit(8),
        name="contributions",
    )(tile_source, own, other, tile_weights, select, labels)


def bulk_fluxes(air, sea):
    shear_u = air[2] - sea[2]
    shear_v = air[3] - sea[3]
    wind_speed = jnp.sqrt(shear_u * shear_u + shear_v * shear_v + 1.0)
    stress_u = 0.8 * wind_speed * shear_u
    stress_v = 0.8 * wind_speed * shear_v
    sensible = 0.6 * wind_speed * (sea[0] - air[0])
    saturated = 0.6 * jnp.exp(0.3 * sea[0]) * (1.0 - 0.1 * jnp.tanh(sea[1]))
    latent = 0.5 * wind_speed * (saturated - air[1])
    return (
        [sensible, latent, -stress_u, -stress_v],
        [-(sensible + latent), latent, stress_u, stress_v],
    )


def flux_kernel(fields, arrived_ref, grid_ref, answer_ref):
    devs, depth, _ = arrived_ref.shape
    per = fields * CAP
    arrived = arrived_ref[...].astype(F32)
    values = arrived[:, :per].reshape(devs * per, TILE).astype(BF16)
    labels = jnp.concatenate([arrived[:, per:]] * (per // 8), axis=1)
    field = lax.broadcasted_iota(jnp.int32, labels.shape, 1) // CAP
    codes = (labels + (field * (2 * XB_DEV)).astype(F32)).reshape(devs * per, TILE)
    codes = jnp.where(labels.reshape(devs * per, TILE) < 0.0, -1.0, codes)
    lane = lax.broadcasted_iota(jnp.int32, (1, TILE), 1)
    side, rest = lane // (fields * XB_DEV), lane % (fields * XB_DEV)
    code_of = side * XB_DEV + rest % XB_DEV + rest // XB_DEV * (2 * XB_DEV)
    hot = jnp.where(codes == code_of.astype(F32), 1.0, 0.0).astype(BF16)
    sums = lax.dot_general(hot, values, (((0,), (0,)), ((), ())), preferred_element_type=F32)
    rows = [sums[XB_DEV * k : XB_DEV * (k + 1)] for k in range(2 * fields)]
    atm_flux, ocn_flux = bulk_fluxes(rows[:fields], rows[fields:])
    table = jnp.concatenate(atm_flux + ocn_flux, axis=0).astype(BF16)
    to = lax.broadcasted_iota(jnp.int32, (TILE, TILE), 0)
    at = lax.broadcasted_iota(jnp.int32, (TILE, TILE), 1)
    both = 2 * fields
    moves = jnp.where(at == to % both * XB_DEV + to // both, 1.0, 0.0).astype(BF16)
    moved = jnp.dot(moves, table, preferred_element_type=F32)
    grid_ref[...] = moved.reshape(XB_DEV, both, TILE).astype(BF16)
    answer = jnp.dot(hot, table, preferred_element_type=F32)
    answer_ref[...] = answer.reshape(devs, per, TILE).astype(BF16)


def fluxes(arrived, fields):
    devs, _, _ = arrived.shape
    return pl.pallas_call(
        functools.partial(flux_kernel, fields),
        out_shape=(
            jax.ShapeDtypeStruct((XB_DEV, 2 * fields, TILE), BF16),
            jax.ShapeDtypeStruct((devs, fields * CAP, TILE), BF16),
        ),
        in_specs=[in_vmem()],
        out_specs=(in_vmem(),) * 2,
        compiler_params=limit(8),
        name="fluxes",
    )(arrived)


def fill_operator(out, grid_ref, links, metric, cols, first_col, all_cols):
    edges = links.shape[0]
    lane = lax.broadcasted_iota(jnp.int32, (edges, TILE), 1)
    away = links[:, cols] - (first_col + lane)
    away = jnp.where(away > all_cols // 2, away - all_cols, away)
    away = jnp.where(away < -(all_cols // 2), away + all_cols, away)
    place = (away + lane).astype(F32)
    value = step_size * metric[:, cols]
    keep = 1.0 - jnp.sum(value, axis=0, keepdims=True)
    place = jnp.concatenate([place, jnp.full((8 - edges, TILE), -1.0e6, F32)], axis=0)
    value = jnp.concatenate([value, jnp.zeros((8 - edges, TILE), F32)], axis=0)
    edge = lax.broadcasted_iota(jnp.int32, (8, TILE), 0)
    whole = value
    for back in range(1, edges):
        same = (pltpu.roll(place, back, 0) == place) & (edge >= back)
        whole = whole + jnp.where(same, pltpu.roll(value, back, 0), 0.0)
    places = [jnp.broadcast_to(place[k : k + 1], (16, TILE)).astype(BF16) for k in range(edges)]
    sums = [jnp.broadcast_to(whole[k : k + 1], (16, TILE)).astype(BF16) for k in range(edges)]
    lanes = lax.broadcasted_iota(jnp.int32, (16, TILE), 1).astype(F32).astype(BF16)
    keep = jnp.broadcast_to(keep, (16, TILE)).astype(BF16)
    for group in range((TILE + 2 * HALO) // 16):
        here = grid_ref[16 * group : 16 * (group + 1)]
        found = jnp.zeros((16, TILE), BF16)
        if HALO <= 16 * group < HALO + TILE:
            found = jnp.where(lanes == here, keep, found)
        for k in range(edges):
            found = jnp.where(places[k] == here, sums[k], found)
        out[16 * group : 16 * (group + 1)] = found


def place_grid(grid_ref):
    grid_ref[...] = (lax.broadcasted_iota(jnp.int32, grid_ref.shape, 0) - HALO).astype(F32).astype(BF16)


def fill_pair(op, grid_ref, links, metric, pair, first_col, all_cols):
    span = TILE + 2 * HALO
    for half in range(2):
        at = (2 * pair + half) * TILE
        cols = pl.ds(pl.multiple_of(at, TILE), TILE)
        lanes = slice(half * TILE, (half + 1) * TILE)
        fill_operator(op.at[half * TILE : half * TILE + span, lanes], grid_ref, links, metric, cols, first_col + at, all_cols)


def clear_corners(op):
    op[TILE + 2 * HALO :, :TILE] = jnp.zeros((TILE, TILE), BF16)
    op[:TILE, TILE:] = jnp.zeros((TILE, TILE), BF16)


def edge_columns(inner_ref, outer_ref, rows, paired):
    inner, outer = inner_ref[rows], outer_ref[rows]
    if not paired:
        return inner, outer
    odd = lax.rem(lax.axis_index("comp"), 2) == 1
    return jnp.where(odd, inner, outer), jnp.where(odd, outer, inner)


def diffuse_kernel(
    all_cols, paired, ocn_hbm, inner_ref, outer_ref, links, metric, base_hbm, edges_hbm, ocn_ref, wide_ref, base_ref,
    edges_ref, even_op, odd_op, grid_ref, in_sems, out_sems, edge_sem,
):
    fields, levels, columns = ocn_ref.shape
    rows = fields * levels
    first = inner_ref.shape[0] - rows
    pairs = columns // (2 * TILE)
    first_col = lax.axis_index("comp") * columns
    parts = in_sems.shape[0]
    wide_cols = columns // parts

    def into(index):
        cols = pl.ds(wide_cols * index, wide_cols)
        return pltpu.make_async_copy(ocn_hbm.at[:, :, cols], ocn_ref.at[:, :, cols], in_sems.at[index])

    def out_of(index):
        cols = pl.ds(pl.multiple_of(4 * TILE * index, TILE), 4 * TILE)
        return pltpu.make_async_copy(base_ref.at[:, cols], base_hbm.at[:, cols], out_sems.at[index])

    for index in range(parts):
        into(index).start()
    edges_ref[0], edges_ref[1] = edge_columns(inner_ref, outer_ref, slice(0, first), paired)
    edges = pltpu.make_async_copy(edges_ref, edges_hbm, edge_sem)
    edges.start()
    place_grid(grid_ref)
    for op in (even_op, odd_op):
        clear_corners(op)
    wide_ref[:, :HALO], wide_ref[:, HALO + columns :] = edge_columns(inner_ref, outer_ref, slice(first, None), paired)

    def narrow(pair):
        at = pl.multiple_of(pair * 2 * TILE, 2 * TILE)
        lands = pl.ds(pl.multiple_of(at + HALO, TILE), 2 * TILE)
        wide_ref[:, lands] = jnp.concatenate(
            [ocn_ref[field, :, pl.ds(at, 2 * TILE)] for field in range(fields)], axis=0
        ).astype(BF16)

    def step(pair, op, next_op, ahead):
        at = pl.multiple_of(pair * 2 * TILE, 2 * TILE)
        done = jnp.dot(wide_ref[:, pl.ds(at, 2 * TILE + 2 * HALO)], op[...], preferred_element_type=F32)
        if next_op is not None:
            fill_pair(next_op, grid_ref, links, metric, pair + 1, first_col, all_cols)
        if ahead:
            narrow(pair + 2)
        base_ref[:, pl.ds(at, 2 * TILE)] = done.astype(BF16)

    fill_pair(even_op, grid_ref, links, metric, 0, first_col, all_cols)
    into(0).wait()
    narrow(0)
    narrow(1)

    def two_pairs(index, carry):
        step(2 * index, even_op, odd_op, True)
        step(2 * index + 1, odd_op, even_op, True)
        out_of(index).start()
        return carry

    for part in range(parts):
        last = part == parts - 1
        if not last:
            into(part + 1).wait()
        per = pairs // 2 // parts
        lax.fori_loop(part * per, (part + 1) * per - last, two_pairs, 0)
    step(pairs - 2, even_op, odd_op, False)
    step(pairs - 1, odd_op, None, False)
    out_of(pairs // 2 - 1).start()
    for index in range(pairs // 2):
        out_of(index).wait()
    edges.wait()


def diffusion(all_cols, paired, ocn_state, inner, outer, links, metric):
    fields, levels, columns = ocn_state.shape
    rows = fields * levels
    edges = (2, inner.shape[0] - rows, HALO)
    return pl.pallas_call(
        functools.partial(diffuse_kernel, all_cols, paired),
        out_shape=(pltpu.HBM((rows, columns), BF16), pltpu.HBM(edges, BF16)),
        in_specs=[in_hbm()] + [in_vmem()] * 4,
        out_specs=(in_hbm(),) * 2,
        scratch_shapes=[
            pltpu.VMEM(ocn_state.shape, F32),
            pltpu.VMEM((rows, columns + 2 * HALO), BF16),
            pltpu.VMEM((rows, columns), BF16),
            pltpu.VMEM(edges, BF16),
            pltpu.VMEM((2 * (TILE + HALO), 2 * TILE), BF16),
            pltpu.VMEM((2 * (TILE + HALO), 2 * TILE), BF16),
            pltpu.VMEM((TILE + 2 * HALO, TILE), BF16),
            pltpu.SemaphoreType.DMA((4,)),
            pltpu.SemaphoreType.DMA((columns // (4 * TILE),)),
            pltpu.SemaphoreType.DMA,
        ],
        compiler_params=limit(12),
        name="diffusion",
    )(outside(ocn_state), inner, outer, links, metric)


def spread_kernel(blocks, source_ref, returned_ref, goes_ref, weight_ref, out_ref, row_ref):
    tiles = weight_ref.shape[0]
    both = out_ref.shape[1]
    devs, per, _ = returned_ref.shape
    stack = returned_ref[...].reshape(devs * per, TILE)
    rows = lax.broadcasted_iota(jnp.int32, (devs * per, goes_ref.shape[1]), 0)
    select = jnp.where(rows == goes_ref[...], 1.0, 0.0).astype(BF16)
    row_ref[...] = lax.dot_general(select, stack, (((0,), (0,)), ((), ())), preferred_element_type=F32)
    out_ref[...] = jnp.zeros_like(out_ref)
    for tile in range(tiles):
        block = lax.rem(source_ref[tile], blocks)
        back = lax.dot_general(
            row_ref[both * tile : both * (tile + 1)].astype(BF16),
            weight_ref[tile],
            (((1,), (1,)), ((), ())),
            preferred_element_type=F32,
        )
        out_ref[block] += back


def spreading(returned, tile_source, tile_weights, goes, blocks, fields):
    tiles = tile_weights.shape[0]
    return pl.pallas_call(
        functools.partial(spread_kernel, blocks),
        out_shape=jax.ShapeDtypeStruct((blocks, 2 * fields, TILE), F32),
        in_specs=[in_smem()] + [in_vmem()] * 3,
        out_specs=in_vmem(),
        scratch_shapes=[pltpu.VMEM((tiles * 2 * fields, TILE), F32)],
        compiler_params=limit(8),
        name="spreading",
    )(tile_source, returned, goes, tile_weights)


def update_kernel(
    all_cols, atm_w_hbm, ocn_w_hbm, ocn_base, atm_hbm, edges_hbm, links_hbm, metric_hbm, own_ref, other_ref, atm_out,
    ocn_out, atm_w, ocn_w, edges_ref, links, metric, wide_ref,
    even_op, odd_op, grid_ref, atm_ref, atm_new, ocn_new, few_sems, in_sems, sems,
):
    levels, _, _ = atm_new.shape
    fields, ocn_levels, columns = ocn_new.shape
    pairs = columns // (2 * TILE)
    twos = pairs // 2
    top = upper_half(fields)
    first_col = lax.axis_index("comp") * columns

    def into(index):
        rows = pl.ds(pl.multiple_of(16 * index, 16), 16)
        return pltpu.make_async_copy(atm_hbm.at[:, rows, :], atm_ref.at[:, rows, :], in_sems.at[index])

    def atm_out_of(index):
        rows = pl.ds(pl.multiple_of(16 * index, 16), 16)
        return pltpu.make_async_copy(atm_new.at[:, rows, :], atm_out.at[:, rows, :], sems.at[index, 0])

    def ocn_out_of(index):
        cols = pl.ds(pl.multiple_of(4 * TILE * index, TILE), 4 * TILE)
        return pltpu.make_async_copy(ocn_new.at[:, :, cols], ocn_out.at[:, :, cols], sems.at[index, 1])

    few = [
        pltpu.make_async_copy(src, dst, few_sems.at[k])
        for k, (src, dst) in enumerate(
            (
                (atm_w_hbm, atm_w),
                (ocn_w_hbm, ocn_w),
                (links_hbm, links),
                (metric_hbm, metric),
                (edges_hbm, edges_ref),
            )
        )
    ]
    for copy in few:
        copy.start()
    for index in range(twos):
        into(index).start()
    for op in (even_op, odd_op):
        clear_corners(op)
    place_grid(grid_ref)

    def narrow(pair):
        lands = pl.ds(pl.multiple_of(pair * 2 * TILE + HALO, TILE), 2 * TILE)
        both = halves(atm_ref, pl.multiple_of(8 * pair, 8), top)
        wide_ref[:, lands] = jnp.concatenate(both, axis=1).astype(BF16)

    def gains(pair):
        return [flux_gain * (own_ref[2 * pair + half] + other_ref[2 * pair + half]) for half in range(2)]

    def ocn_step(index):
        for pair in (2 * index, 2 * index + 1):
            flux = gains(pair)
            for half in range(2):
                cols = pl.ds(pl.multiple_of((2 * pair + half) * TILE, TILE), TILE)
                base = ocn_base[:, cols].astype(F32)
                for field in range(fields):
                    ocn_new[field, :, cols] = (
                        base[field * ocn_levels : (field + 1) * ocn_levels]
                        + ocn_w[...] * flux[half][fields + field : fields + field + 1]
                    )
        ocn_out_of(index).start()

    def atm_step(pair, op, next_op, ahead):
        at = pl.multiple_of(pair * 2 * TILE, 2 * TILE)
        flux = gains(pair)
        done = jnp.dot(wide_ref[:, pl.ds(at, 2 * TILE + 2 * HALO)], op[...], preferred_element_type=F32)
        if next_op is not None:
            fill_pair(next_op, grid_ref, links, metric, pair + 1, first_col, all_cols)
        if ahead:
            narrow(pair + 2)
        gain = jnp.concatenate([flux[0][:fields], flux[1][:fields]], axis=0)
        rows = pl.ds(pl.multiple_of(8 * pair, 8), 8)
        for level in range(0, levels, 2):
            here = done[level * fields : level * fields + 8]
            low = jnp.where(top, here[:, :TILE], turned(here[:, TILE:]))
            high = jnp.where(top, turned(here[:, :TILE]), here[:, TILE:])
            atm_new[level, rows, :] = low + atm_w[level : level + 1] * gain
            atm_new[level + 1, rows, :] = high + atm_w[level + 1 : level + 2] * gain

    lead = min(2, twos)
    for copy in few[:2]:
        copy.wait()
    for index in range(lead):
        ocn_step(index)
    for copy in few[2:]:
        copy.wait()
    wide_ref[:, :HALO] = edges_ref[0]
    wide_ref[:, HALO + columns :] = edges_ref[1]
    fill_pair(even_op, grid_ref, links, metric, 0, first_col, all_cols)
    into(0).wait()
    narrow(0)
    narrow(1)

    def two_pairs(index, carry):
        into(index + 1).wait()
        atm_step(2 * index, even_op, odd_op, True)
        atm_step(2 * index + 1, odd_op, even_op, True)
        atm_out_of(index).start()

        @pl.when(index + lead < twos)
        def _():
            ocn_step(index + lead)

        return carry

    lax.fori_loop(0, twos - 1, two_pairs, 0)
    atm_step(pairs - 2, even_op, odd_op, False)
    atm_step(pairs - 1, odd_op, None, False)
    atm_out_of(twos - 1).start()
    for index in range(twos):
        atm_out_of(index).wait()
        ocn_out_of(index).wait()


def update(all_cols, atm_wide, ocn_wide, ocn_base, atm_rows, edges, links, metric, own, other):
    levels, count, _ = atm_rows.shape
    ocn_levels, columns = ocn_wide.shape[0], links.shape[1]
    fields = own.shape[1] // 2
    ocn_shape = (fields, ocn_levels, columns)
    return pl.pallas_call(
        functools.partial(update_kernel, all_cols),
        out_shape=(pltpu.HBM(atm_rows.shape, F32), pltpu.HBM(ocn_shape, F32)),
        in_specs=[in_hbm()] * 2 + [in_vmem()] + [in_hbm()] * 4 + [in_vmem()] * 2,
        out_specs=(in_hbm(),) * 2,
        scratch_shapes=[
            pltpu.VMEM(atm_wide.shape, F32),
            pltpu.VMEM(ocn_wide.shape, F32),
            pltpu.VMEM(edges.shape, BF16),
            pltpu.VMEM(links.shape, links.dtype),
            pltpu.VMEM(metric.shape, F32),
            pltpu.VMEM((fields * levels, columns + 2 * HALO), BF16),
            pltpu.VMEM((2 * (TILE + HALO), 2 * TILE), BF16),
            pltpu.VMEM((2 * (TILE + HALO), 2 * TILE), BF16),
            pltpu.VMEM((TILE + 2 * HALO, TILE), BF16),
            pltpu.VMEM(atm_rows.shape, F32),
            pltpu.VMEM(atm_rows.shape, F32),
            pltpu.VMEM(ocn_shape, F32),
            pltpu.SemaphoreType.DMA((5,)),
            pltpu.SemaphoreType.DMA((columns // (4 * TILE),)),
            pltpu.SemaphoreType.DMA((columns // (4 * TILE), 2)),
        ],
        compiler_params=limit(20),
        name="update",
    )(
        outside(atm_wide), outside(ocn_wide), ocn_base, outside(atm_rows), outside(edges), outside(links),
        outside(metric), own, other,
    )


def exchanged(inner, outer, axis):
    count = lax.axis_size(axis)
    if count % 2:
        onward = [(i, (i + 1) % count) for i in range(count)]
        return lax.ppermute(inner, axis, onward), lax.ppermute(outer, axis, [(j, i) for i, j in onward])
    within = [(i, i ^ 1) for i in range(count)]
    across = [(i, (i - 1 if i % 2 == 0 else i + 1) % count) for i in range(count)]
    return lax.ppermute(inner, axis, within), lax.ppermute(outer, axis, across)


def routes(tile_source, tile_target, owner_map, blocks, fields, dev_count):
    tiles = tile_source.shape[0]
    xblocks = owner_map.shape[0]
    per = fields * CAP
    matched = tile_target[:, None] == jnp.arange(xblocks, dtype=jnp.int32)[None, :]
    placed_at = jnp.sum(jnp.where(matched, owner_map[None, :], 0), axis=1)
    owner = placed_at // XB_DEV
    side = (tile_source >= blocks).astype(jnp.int32)
    segment = side * XB_DEV + placed_at % XB_DEV
    index = jnp.arange(tiles, dtype=jnp.int32)
    before = (index[None, :] < index[:, None]) & (owner[None, :] == owner[:, None])
    rank = jnp.sum(before.astype(jnp.int32), axis=1)
    slots = jnp.arange(dev_count * 8, dtype=jnp.int32)
    at_slot = (slots[:, None] // 8 == owner[None, :]) & (slots[:, None] % CAP == rank[None, :])
    label = jnp.sum(jnp.where(at_slot, segment[None, :] + 1, 0), axis=1) - 1
    labels = jnp.broadcast_to(label.astype(F32)[:, None], (dev_count * 8, TILE)).reshape(dev_count, 8, TILE)
    column = jnp.arange(tiles * 2 * fields, dtype=jnp.int32)
    mine = column[:, None] // (2 * fields) == index[None, :]
    packed = jnp.sum(jnp.where(mine, (2 * (owner * per + rank) + side)[None, :], 0), axis=1)
    goes = jnp.where(
        packed % 2 == column // fields % 2, packed // 2 + column % fields * CAP, -1
    )
    rows = jnp.arange(dev_count * per, dtype=jnp.int32)
    to_slots = (rows[:, None] == goes[None, :]).astype(BF16)
    return labels, to_slots, goes[None, :]


def shards(
    atm_state,
    ocn_state,
    atm_weights,
    ocn_weights,
    atm_metric,
    ocn_metric,
    atm_links,
    ocn_links,
    tile_weights,
    tile_source,
    tile_target,
    owner_map,
):
    comp_count = lax.axis_size("comp")
    dev_count = comp_count * lax.axis_size("lev")
    fields, _, columns = atm_state.shape
    blocks = columns // TILE
    swap = [(0, 1), (1, 0)]

    paired = comp_count % 2 == 0
    part, inner, outer, atm_wide, ocn_wide = surface(
        to_rows(atm_state), ocn_state, atm_weights, ocn_weights, paired
    )
    part_other = lax.ppermute(part, "lev", swap)
    labels, to_slots, goes = routes(tile_source, tile_target, owner_map, blocks, fields, dev_count)
    outgoing = contributions(part, part_other, tile_source, tile_weights, to_slots, labels)
    outgoing, inner, outer = lax.optimization_barrier((outgoing, inner, outer))
    arrived = lax.all_to_all(outgoing, BOTH, split_axis=0, concat_axis=0, tiled=True)
    inner, outer = exchanged(inner, outer, "comp")
    xgrid, answer = fluxes(arrived, fields)
    answer, links = lax.optimization_barrier((answer, ocn_links))
    returned = lax.all_to_all(answer, BOTH, split_axis=0, concat_axis=0, tiled=True)
    all_cols = columns * comp_count
    ocn_base, edges = diffusion(all_cols, paired, ocn_state, inner, outer, links, ocn_metric)
    returned, ocn_base, edges = lax.optimization_barrier((returned, ocn_base, edges))
    spread = spreading(returned, tile_source, tile_weights, goes, blocks, fields)
    spread_other = lax.ppermute(spread, "lev", swap)
    atm_new, ocn_new = update(
        all_cols, atm_wide, ocn_wide, ocn_base, to_rows(atm_state), edges, atm_links, atm_metric, spread, spread_other
    )
    return (from_rows(atm_new, fields), ocn_new, xgrid)


def solution(mesh):
    placed = (
        P(None, "lev", ("grp", "comp")),
        P(None, "lev", ("grp", "comp")),
        P("lev"),
        P("lev"),
        P(None, "comp"),
        P(None, "comp"),
        P(None, "comp"),
        P(None, "comp"),
        P(("comp", "lev"), None, None),
        P(("comp", "lev")),
        P(("comp", "lev")),
        P(),
    )
    return jax.shard_map(
        shards,
        mesh=mesh,
        in_specs=placed,
        out_specs=(
            P(None, "lev", ("grp", "comp")),
            P(None, "lev", ("grp", "comp")),
            P(("grp", "comp", "lev"), None, None),
        ),
        check_vma=False,
    )
```
